32 devices in a mesh: gx: 2 (over y), gy: 4 (over z), gz: 4 (over x, core).
Axes of the slice: x: 2, y: 2, z: 4, core: 2. Of those that a mesh axis runs over, the one named last changes fastest.
Arguments:
- right_side: float32 [32, 64, 512], P('gx', 'gy', 'gz'), may hold values from -5 to 5, as said below
- conductivity: float32 [32, 64, 512], P('gx', 'gy', 'gz'), may hold values from 0.1 to 10
Outputs:
- solution: float32 [32, 64, 512], P('gx', 'gy', 'gz')
The draws below stay inside these ranges and needn't reach their ends.
Inputs may be any that keep to these rules, and one draw needn't show every extreme that they name: `right_side`: a source field of order one.
All inputs are finite; a program needn't handle non-finite values.
Results may differ from the reference program's by a relative error of at most 0.0001.
Values sent between devices are 32-bit elements; how exact they have to be, the bound alone decides.
A program may use at most 64 MiB of HBM per device.

```python
import math
import jax
import jax.numpy as jnp

COARSE = 8
SWEEPS = 4
CSWEEPS = 8
CYCLES = 2
NX = 32
NY = 64
NZ = 512


def spread_ends(values):
    highest = jnp.maximum(jnp.max(values), 0.5)
    lowest = jnp.maximum(-jnp.min(values), 0.5)
    scaled = jnp.where(values > 0, values * (5.0 / highest), values * (5.0 / lowest))
    return jnp.clip(scaled, -5.0, 5.0)


def draw_right_side(key, part):
    values = jax.random.normal(key, (NX, NY, NZ), jnp.float32)
    return spread_ends(values)


def steps_of(own_key, shape, cuts, smallest, high):
    factor_of, own = 1.0, jax.random.fold_in(own_key, 6)
    for dim, shards_of in cuts:
        heights = jnp.exp(jax.random.uniform(jax.random.fold_in(own, dim), (shards_of,), jnp.float32, smallest / len(cuts), high / len(cuts)))
        factor_of = factor_of * jnp.repeat(heights, shape[dim] // shards_of).reshape([-1 if axis == dim else 1 for axis in range(len(shape))])
    return factor_of


def setup_inputs(seed: int = 0) -> dict:
    streams_of = jax.random.split(jax.random.key(seed), 3)
    return {
        "right_side": draw_right_side(jax.random.fold_in(streams_of[2], 71), 0),
        "conductivity": jnp.clip(jnp.exp(math.log(10.0) - 4.6051702 * jax.random.uniform(streams_of[1], (NX, NY, NZ), jnp.float32) ** steps_of(streams_of[1], (NX, NY, NZ), ((0, 2), (1, 4), (2, 4)), -0.2, 0.2)), 0.1, 10.0),
    }


omega_weight = 0.8


def stencil_coefs(conduct):
    padded = jnp.pad(conduct, 1)
    face_west = 0.5 * (conduct + padded[:-2, 1:-1, 1:-1])
    face_east = 0.5 * (conduct + padded[2:, 1:-1, 1:-1])
    face_south = 0.5 * (conduct + padded[1:-1, :-2, 1:-1])
    face_north = 0.5 * (conduct + padded[1:-1, 2:, 1:-1])
    face_below = 0.5 * (conduct + padded[1:-1, 1:-1, :-2])
    face_above = 0.5 * (conduct + padded[1:-1, 1:-1, 2:])
    diagonal = ((face_west + face_east) + (face_south + face_north)) + (face_below + face_above)
    return (face_west, face_east, face_south, face_north, face_below, face_above, diagonal)


def apply_operator(values, stencil):
    face_west, face_east, face_south, face_north, face_below, face_above, diagonal = stencil
    padded = jnp.pad(values, 1)
    nearby = face_west * padded[:-2, 1:-1, 1:-1] + face_east * padded[2:, 1:-1, 1:-1]
    nearby = nearby + face_south * padded[1:-1, :-2, 1:-1] + face_north * padded[1:-1, 2:, 1:-1]
    nearby = nearby + face_below * padded[1:-1, 1:-1, :-2] + face_above * padded[1:-1, 1:-1, 2:]
    return diagonal * values - nearby


def jacobi(values, source, stencil, inside, repeats):
    safe_diag = jnp.where(inside, stencil[6], 1.0)
    for sweep_step in range(repeats):
        update = values + omega_weight * (source - apply_operator(values, stencil)) / safe_diag
        values = jnp.where(inside, update, 0.0)
    return values


def restrict(values, factor):
    extent = values.shape
    blocks = values.reshape(extent[0] // factor, factor, extent[1] // factor, factor, extent[2] // factor, factor)
    return blocks.sum(axis=(1, 3, 5))


def prolong(values, factor):
    extent = values.shape
    spread = jnp.broadcast_to(values[:, None, :, None, :, None], (extent[0], factor, extent[1], factor, extent[2], factor))
    return spread.reshape(extent[0] * factor, extent[1] * factor, extent[2] * factor)


def reference(right_side, conductivity):
    stencil = stencil_coefs(conductivity)
    coarse_stencil = stencil_coefs(restrict(conductivity, COARSE) / (COARSE * COARSE))
    solution = jnp.zeros_like(right_side)
    for cycle_step in range(CYCLES):
        solution = jacobi(solution, right_side, stencil, True, SWEEPS)
        residual = right_side - apply_operator(solution, stencil)
        coarse_rhs = restrict(residual, COARSE)
        correction = jacobi(jnp.zeros_like(coarse_rhs), coarse_rhs, coarse_stencil, True, CSWEEPS)
        solution = solution + prolong(correction, COARSE)
        solution = jacobi(solution, right_side, stencil, True, SWEEPS)
    return solution
```

```python
import functools

import jax
import jax.numpy as jnp
from jax import lax
from jax.experimental import pallas as pl
from jax.experimental.pallas import tpu as pltpu
from jax.sharding import PartitionSpec as P

COARSE = 8
SWEEPS = 4
CSWEEPS = 8
CYCLES = 2
OMEGA = 0.8
LANES = 128
ROWS = 8
DEPTH = SWEEPS + 1
MESH = pl.DeviceIdType.MESH
F32 = jnp.float32
HIGH = lax.Precision.HIGHEST


def kernel(
    counts, block, s_ref, c_ref, o_ref,
    cs, fresh, work_a, work_b, coef, scale, pack_cs, land_cs, pack_v, land_v,
    line, plane, coarse, spread,
    send_sem, recv_sem, line_send, line_recv, plane_send, plane_recv,
):
    nx, ny, nz = counts
    bx, by, bz = block
    px, py = bx + 2 * DEPTH, by + 2 * ROWS
    cx, cy, cz = bx // COARSE, by // COARSE, bz // COARSE
    ypad = line.shape[-2]
    mx, my, mz = lax.axis_index("gx"), lax.axis_index("gy"), lax.axis_index("gz")
    mine = (mx, my, mz)

    def present(offset):
        ok = None
        for here, step, size in zip(mine, offset, counts):
            if step == 0:
                continue
            good = here + step < size if step > 0 else here + step >= 0
            ok = good if ok is None else ok & good
        return ok

    def device(offset):
        return {
            "gx": mx + offset[0], "gy": my + offset[1], "gz": mz + offset[2]
        }

    offsets = [
        (dx, dy, dz)
        for dx in (-1, 0, 1) for dy in (-1, 0, 1) for dz in (-1, 0, 1)
        if (dx, dy, dz) != (0, 0, 0)
        and (dx == 0 or nx > 1) and (dy == 0 or ny > 1) and (dz == 0 or nz > 1)
    ]
    flat = [o for o in offsets if o[2] == 0]
    deep = [o for o in offsets if o[2] != 0]
    number = {o: i for i, o in enumerate(offsets)}

    cs[...] = jnp.zeros_like(cs)
    fresh[...] = jnp.zeros_like(fresh)
    land_cs[...] = jnp.zeros_like(land_cs)
    land_v[...] = jnp.zeros_like(land_v)

    barrier = pltpu.get_barrier_semaphore()
    total = jnp.int32(0)
    for o in offsets:
        ok = present(o)
        total = total + ok.astype(jnp.int32)

        @pl.when(ok)
        def _():
            pl.semaphore_signal(barrier, inc=1, device_id=device(o), device_id_type=MESH)

    for k in range(nz):
        far = jnp.abs(mz - k) >= 2
        total = total + far.astype(jnp.int32)

        @pl.when(far)
        def _():
            pl.semaphore_signal(
                barrier, inc=1, device_id={"gx": mx, "gy": my, "gz": k}, device_id_type=MESH
            )

    for i in range(nx):
        for j in range(ny):
            far = (jnp.abs(mx - i) >= 2) | (jnp.abs(my - j) >= 2)
            total = total + far.astype(jnp.int32)

            @pl.when(far)
            def _():
                pl.semaphore_signal(
                    barrier, inc=1, device_id={"gx": i, "gy": j, "gz": mz}, device_id_type=MESH
                )

    pl.semaphore_wait(barrier, total)

    lane = lax.broadcasted_iota(jnp.int32, (py, LANES), 1)
    lane_by = lax.broadcasted_iota(jnp.int32, (by, LANES), 1)

    xs = {0: pl.ds(DEPTH, bx), 1: pl.ds(bx, DEPTH), -1: pl.ds(DEPTH, DEPTH)}
    xd = {0: pl.ds(DEPTH, bx), 1: pl.ds(0, DEPTH), -1: pl.ds(DEPTH + bx, DEPTH)}
    ys = {0: pl.ds(ROWS, by), 1: pl.ds(by, ROWS), -1: pl.ds(ROWS, ROWS)}
    yd = {0: pl.ds(ROWS, by), 1: pl.ds(0, ROWS), -1: pl.ds(ROWS + by, ROWS)}
    yp = {0: pl.ds(0, by), 1: pl.ds(by - ROWS, ROWS), -1: pl.ds(0, ROWS)}

    def copy(which, o, main, packed, landed):
        dx, dy, dz = o
        if dz == 0:
            source, target = main.at[:, xs[dx], ys[dy]], main.at[:, xd[dx], yd[dy]]
        else:
            side = 0 if dz > 0 else 1
            source = packed.at[side, :, yp[dy]]
            target = landed.at[dx + 1, side, :, yd[dy]]
        return pltpu.make_async_remote_copy(
            src_ref=source, dst_ref=target,
            send_sem=send_sem.at[which, number[o]], recv_sem=recv_sem.at[which, number[o]],
            device_id=device(o), device_id_type=MESH,
        )

    def send_flat(which, main, packed, landed):
        for o in flat:
            @pl.when(present(o))
            def _():
                copy(which, o, main, packed, landed).start()

    def send_deep(which, main, packed, landed):
        for f in range(packed.shape[1]):
            right = jnp.zeros((by, LANES), F32)
            left = jnp.zeros((by, LANES), F32)
            for j in range(bx):
                v = main[f, DEPTH + j, ROWS:ROWS + by]
                here = lane_by // ROWS == j
                right = jnp.where(here, pltpu.roll(v, (ROWS * j + ROWS) % LANES, 1), right)
                left = jnp.where(here, pltpu.roll(v, (ROWS * j) % LANES, 1), left)
            packed[0, f] = right
            packed[1, f] = left
        for o in deep:
            @pl.when(present(o))
            def _():
                copy(which, o, main, packed, landed).start()

    def arrive(which, main, packed, landed):
        for o in flat + deep:
            @pl.when(present(tuple(-step for step in o)))
            def _():
                copy(which, o, main, packed, landed).wait_recv()

    def sent(which, main, packed, landed):
        for o in flat + deep:
            @pl.when(present(o))
            def _():
                copy(which, o, main, packed, landed).wait_send()

    def rim_of(landed, f, x):
        if x < DEPTH:
            slot, j = 2, bx - DEPTH + x
        elif x < DEPTH + bx:
            slot, j = 1, x - DEPTH
        else:
            slot, j = 0, x - DEPTH - bx
        before = pltpu.roll(landed[slot, 0, f], (LANES - ROWS - ROWS * j) % LANES, 1)
        after = pltpu.roll(landed[slot, 1, f], (LANES - ROWS * j) % LANES, 1)
        return jnp.where(
            lane < ROWS, after, jnp.where(lane >= LANES - ROWS, before, 0.0)
        )

    def line_copy(k, p):
        return pltpu.make_async_remote_copy(
            src_ref=line.at[k, mz], dst_ref=line.at[k, mz],
            send_sem=line_send.at[k, p], recv_sem=line_recv.at[k, mz],
            device_id={"gx": mx, "gy": my, "gz": p}, device_id_type=MESH,
        )

    def plane_copy(k, i, j):
        return pltpu.make_async_remote_copy(
            src_ref=plane.at[k, mx, my], dst_ref=plane.at[k, mx, my],
            send_sem=plane_send.at[k, i, j], recv_sem=plane_recv.at[k, mx, my],
            device_id={"gx": i, "gy": j, "gz": mz}, device_id_type=MESH,
        )

    def restrict_send(k, sums):
        row = lax.broadcasted_iota(jnp.int32, (ypad, LANES), 0)
        parts = []
        for a in range(cx):
            out = jnp.zeros((ypad, LANES), F32)
            for b in range(cy):
                t = jnp.sum(sums[a][b * COARSE:(b + 1) * COARSE], axis=0, keepdims=True)
                out = jnp.where(row == my * cy + b, t, out)
            parts.append(out)
        tall = jnp.concatenate(parts, axis=0)
        fine = lax.broadcasted_iota(jnp.int32, (bz, LANES), 0)
        cell = lax.broadcasted_iota(jnp.int32, (bz, LANES), 1)
        place = (cell == mz * cz + fine // COARSE).astype(F32)
        tall = jnp.dot(tall, place, preferred_element_type=F32, precision=HIGH)
        line[k, mz] = tall.reshape(cx, ypad, LANES)
        for p in range(nz):
            @pl.when(p != mz)
            def _():
                line_copy(k, p).start()

    def gather_middle(k):
        for p in range(nz):
            @pl.when(p != mz)
            def _():
                pltpu.make_async_remote_copy(
                    src_ref=line.at[k, p], dst_ref=line.at[k, p],
                    send_sem=line_send.at[k, p], recv_sem=line_recv.at[k, p],
                    device_id={"gx": mx, "gy": my, "gz": p}, device_id_type=MESH,
                ).wait_recv()
        acc = line[k, 0]
        for p in range(1, nz):
            acc = acc + line[k, p]
        plane[k, mx, my] = acc
        for i in range(nx):
            for j in range(ny):
                @pl.when((i != mx) | (j != my))
                def _():
                    plane_copy(k, i, j).start()

    def gather_end(k):
        for i in range(nx):
            for j in range(ny):
                @pl.when((i != mx) | (j != my))
                def _():
                    pltpu.make_async_remote_copy(
                        src_ref=plane.at[k, i, j], dst_ref=plane.at[k, i, j],
                        send_sem=plane_send.at[k, i, j], recv_sem=plane_recv.at[k, i, j],
                        device_id={"gx": i, "gy": j, "gz": mz}, device_id_type=MESH,
                    ).wait_recv()
        parts = []
        for i in range(nx):
            acc = plane[k, i, 0]
            for j in range(1, ny):
                acc = acc + plane[k, i, j]
            parts.append(acc)
        return jnp.concatenate(parts, axis=0)

    def gather_sent(k):
        for p in range(nz):
            @pl.when(p != mz)
            def _():
                line_copy(k, p).wait_send()
        for i in range(nx):
            for j in range(ny):
                @pl.when((i != mx) | (j != my))
                def _():
                    plane_copy(k, i, j).wait_send()

    def six(get, x):
        main, rim = get(0, x), get(1, x)
        m_up, m_down = pltpu.roll(main, 1, 1), pltpu.roll(main, LANES - 1, 1)
        r_up, r_down = pltpu.roll(rim, 1, 1), pltpu.roll(rim, LANES - 1, 1)
        out = []
        for part, v in ((0, main), (1, rim)):
            low = jnp.where(lane == 0, r_up, m_up) if part == 0 else jnp.where(lane == 0, m_up, r_up)
            high = (
                jnp.where(lane == LANES - 1, r_down, m_down) if part == 0
                else jnp.where(lane == LANES - 1, m_down, r_down)
            )
            out.append((v, (
                get(part, x - 1), get(part, x + 1),
                pltpu.roll(v, 1, 0), pltpu.roll(v, py - 1, 0), low, high,
            )))
        return out

    def sweep(source, target, margin):
        def step(x, carry):
            for part, (v, near) in enumerate(six(lambda p, i: source[p, i], x)):
                acc = (1.0 - OMEGA) * v + coef[6, part, x]
                for n in range(6):
                    acc = acc + coef[n, part, x] * near[n]
                target[part, x] = acc
            return carry
        lax.fori_loop(margin, px - margin, step, 0)

    def core(source, x, weight):
        inner = slice(ROWS, ROWS + by)
        v = source[0, x]
        rim = source[1, x, inner]
        mid = v[inner]
        low = jnp.where(lane_by == 0, pltpu.roll(rim, 1, 1), pltpu.roll(mid, 1, 1))
        high = jnp.where(
            lane_by == LANES - 1, pltpu.roll(rim, LANES - 1, 1), pltpu.roll(mid, LANES - 1, 1)
        )
        near = (
            source[0, x - 1, inner], source[0, x + 1, inner],
            pltpu.roll(v, 1, 0)[inner], pltpu.roll(v, py - 1, 0)[inner], low, high,
        )
        acc = weight * mid + coef[6, 0, x, inner]
        for n in range(6):
            acc = acc + coef[n, 0, x, inner] * near[n]
        return acc

    cs[0, 0, DEPTH:DEPTH + bx, ROWS:ROWS + by] = c_ref[...]
    cs[0, 1, DEPTH:DEPTH + bx, ROWS:ROWS + by] = s_ref[...]
    both = cs.at[0]
    send_flat(0, both, pack_cs, land_cs)
    send_deep(0, both, pack_cs, land_cs)

    sums = []
    for a in range(cx):
        acc = c_ref[a * COARSE]
        for t in range(1, COARSE):
            acc = acc + c_ref[a * COARSE + t]
        sums.append(acc * (1.0 / (COARSE * COARSE)))
    restrict_send(0, sums)
    spread[...] = jnp.zeros_like(spread)
    gather_middle(0)
    arrive(0, both, pack_cs, land_cs)

    for f in range(2):
        for x in range(px):
            cs[1, f, x] = rim_of(land_cs, f, x)

    def make(x, carry):
        for part, (c, near) in enumerate(six(lambda p, i: cs[p, 0, i], x)):
            faces = [0.5 * (c + n) for n in near]
            diag = (faces[0] + faces[1]) + (faces[2] + faces[3]) + (faces[4] + faces[5])
            here = c > 0.0
            w = jnp.where(here, OMEGA / jnp.where(here, diag, 1.0), 0.0)
            for n in range(6):
                coef[n, part, x] = w * faces[n]
            first = w * cs[part, 1, x]
            coef[6, part, x] = first
            work_a[part, x] = first
            if part == 0:
                scale[x] = (1.0 / OMEGA) * diag
        return carry
    lax.fori_loop(1, px - 1, make, 0)

    for cycle in range(CYCLES):
        if cycle == 0:
            order, first = [(work_a, work_b), (work_b, work_a), (work_a, work_b)], 2
        else:
            order, first = [(work_a, work_b), (work_b, work_a)] * 2, 1
        for i, (source, target) in enumerate(order):
            sweep(source, target, first + i)
        last = order[-1][1]
        which = 1 + 2 * cycle
        slot = which - 1
        main, packed, landed = fresh.at[slot], pack_v.at[slot], land_v.at[slot]
        fresh[slot, 0, DEPTH:DEPTH + bx, ROWS:ROWS + by] = (
            last[0, DEPTH:DEPTH + bx, ROWS:ROWS + by]
        )

        sums = []
        for a in range(cx):
            def add(t, acc):
                x = DEPTH + a * COARSE + t
                return acc + core(last, x, -OMEGA) * scale[x, ROWS:ROWS + by]
            sums.append(lax.fori_loop(0, COARSE, add, jnp.zeros((by, LANES), F32)))
        restrict_send(1 + cycle, sums)
        send_flat(which, main, packed, landed)
        send_deep(which, main, packed, landed)
        gather_middle(1 + cycle)

        if cycle == 0:
            cc = gather_end(0)
            shape = cc.shape
            row = lax.broadcasted_iota(jnp.int32, shape, 1)
            col = lax.broadcasted_iota(jnp.int32, shape, 2)
            blank = jnp.zeros((1,) + shape[1:], F32)

            def shifts(v):
                return (
                    jnp.concatenate([blank, v[:-1]], axis=0),
                    jnp.concatenate([v[1:], blank], axis=0),
                    jnp.where(row == 0, 0.0, pltpu.roll(v, 1, 1)),
                    jnp.where(row == shape[1] - 1, 0.0, pltpu.roll(v, shape[1] - 1, 1)),
                    jnp.where(col == 0, 0.0, pltpu.roll(v, 1, 2)),
                    jnp.where(col == LANES - 1, 0.0, pltpu.roll(v, LANES - 1, 2)),
                )

            faces = [0.5 * (cc + n) for n in shifts(cc)]
            diag = (faces[0] + faces[1]) + (faces[2] + faces[3]) + (faces[4] + faces[5])
            here = cc > 0.0
            w = jnp.where(here, OMEGA / jnp.where(here, diag, 1.0), 0.0)
            for n in range(6):
                coarse[n] = w * faces[n]
            coarse[6] = w

        rhs = gather_end(1 + cycle) * coarse[6]
        corr = rhs
        for _ in range(CSWEEPS - 1):
            acc = (1.0 - OMEGA) * corr + rhs
            for n, v in enumerate(shifts(corr)):
                acc = acc + coarse[n] * v
            corr = acc

        tall = corr.reshape(-1, LANES)
        cell = lax.broadcasted_iota(jnp.int32, (LANES, LANES), 0)
        fine = lax.broadcasted_iota(jnp.int32, (LANES, LANES), 1)
        to_main = (cell == mz * cz + fine // COARSE).astype(F32)
        to_rim = (
            ((fine < ROWS) & (cell == mz * cz + cz))
            | ((fine >= LANES - ROWS) & (cell == mz * cz - 1))
        ).astype(F32)
        for part, matrix in ((0, to_main), (1, to_rim)):
            wide = jnp.dot(tall, matrix, preferred_element_type=F32, precision=HIGH)
            spread[part, 1:1 + shape[0], ROWS:ROWS + shape[1]] = wide.reshape(shape)

        def lifted(part, x):
            a = mx * cx + 1 + (x - DEPTH) // COARSE
            rows = []
            for t in range(py // ROWS):
                one = spread[part, a, pl.ds(ROWS - 1 + my * cy + t, 1)]
                rows.append(jnp.broadcast_to(one, (ROWS, LANES)))
            return jnp.concatenate(rows, axis=0)

        lifts = {}
        for x in range(px):
            key = (x - DEPTH) // COARSE
            if key not in lifts:
                lifts[key] = (lifted(0, x), lifted(1, x))
        arrive(which, main, packed, landed)
        for x in range(px):
            key = (x - DEPTH) // COARSE
            work_a[0, x] = fresh[slot, 0, x] + lifts[key][0]
            work_a[1, x] = rim_of(land_v.at[slot], 0, x) + lifts[key][1]

        sweep(work_a, work_b, 1)
        sweep(work_b, work_a, 2)
        sweep(work_a, work_b, 3)
        if cycle == CYCLES - 1:
            def finish(x, carry):
                o_ref[x - DEPTH] = core(work_b, x, 1.0 - OMEGA)
                return carry
            lax.fori_loop(DEPTH, DEPTH + bx, finish, 0)
        else:
            which, slot = which + 1, slot + 1
            main, packed, landed = fresh.at[slot], pack_v.at[slot], land_v.at[slot]

            def finish(x, carry):
                fresh[slot, 0, x, ROWS:ROWS + by] = core(work_b, x, 1.0 - OMEGA)
                return carry
            lax.fori_loop(DEPTH, DEPTH + bx, finish, 0)
            send_flat(which, main, packed, landed)
            send_deep(which, main, packed, landed)
            arrive(which, main, packed, landed)
            for x in range(px):
                work_a[0, x] = fresh[slot, 0, x]
                work_a[1, x] = rim_of(land_v.at[slot], 0, x)

    sent(0, both, pack_cs, land_cs)
    for k in range(2 * CYCLES - 1):
        sent(1 + k, fresh.at[k], pack_v.at[k], land_v.at[k])
    for k in range(CYCLES + 1):
        gather_sent(k)


def body(counts, right_side, conductivity):
    nx, ny, nz = counts
    bx, by, bz = block = right_side.shape
    assert bz == LANES and bx * ROWS <= LANES and bx % COARSE == 0 and by % COARSE == 0
    assert nz * bz // COARSE <= LANES
    px, py = bx + 2 * DEPTH, by + 2 * ROWS
    cx = bx // COARSE
    ypad = -(-(ny * by // COARSE) // ROWS) * ROWS
    moves = 2 * CYCLES - 1
    vmem = pltpu.VMEM
    dma = pltpu.SemaphoreType.DMA
    return pl.pallas_call(
        functools.partial(kernel, counts, block),
        out_shape=jax.ShapeDtypeStruct(block, F32),
        in_specs=[pl.BlockSpec(memory_space=vmem)] * 2,
        out_specs=pl.BlockSpec(memory_space=vmem),
        scratch_shapes=[
            vmem((2, 2, px, py, LANES), F32),
            vmem((moves, 1, px, py, LANES), F32),
            vmem((2, px, py, LANES), F32),
            vmem((2, px, py, LANES), F32),
            vmem((7, 2, px, py, LANES), F32),
            vmem((px, py, LANES), F32),
            vmem((2, 2, by, LANES), F32),
            vmem((3, 2, 2, py, LANES), F32),
            vmem((moves, 2, 1, by, LANES), F32),
            vmem((moves, 3, 2, 1, py, LANES), F32),
            vmem((CYCLES + 1, nz, cx, ypad, LANES), F32),
            vmem((CYCLES + 1, nx, ny, cx, ypad, LANES), F32),
            vmem((7, nx * cx, ypad, LANES), F32),
            vmem((2, nx * cx + 2, ypad + 2 * ROWS, LANES), F32),
            dma((moves + 1, 26)),
            dma((moves + 1, 26)),
            dma((CYCLES + 1, nz)),
            dma((CYCLES + 1, nz)),
            dma((CYCLES + 1, nx, ny)),
            dma((CYCLES + 1, nx, ny)),
        ],
        compiler_params=pltpu.CompilerParams(
            collective_id=0, has_side_effects=True, vmem_limit_bytes=40 * 1024 * 1024
        ),
    )(right_side, conductivity)


def solution(mesh):
    counts = tuple(mesh.shape[name] for name in ("gx", "gy", "gz"))
    return jax.shard_map(
        functools.partial(body, counts),
        mesh=mesh,
        in_specs=(P("gx", "gy", "gz"), P("gx", "gy", "gz")),
        out_specs=P("gx", "gy", "gz"),
        check_vma=False,
    )
```

```python
import functools

import jax
import jax.numpy as jnp
from jax import lax
from jax.experimental import pallas as pl
from jax.experimental.pallas import tpu as pltpu
from jax.sharding import PartitionSpec as P

COARSE = 8
SWEEPS = 4
CSWEEPS = 8
CYCLES = 2
OMEGA = 0.8
LANES = 128
ROWS = 8
DEPTH = SWEEPS + 1
MESH = pl.DeviceIdType.MESH
F32 = jnp.float32
HIGH = lax.Precision.HIGHEST


def kernel(
    counts, block, s_ref, c_ref, o_ref,
    cs, fresh, work_a, work_b, coef, scale, pack_cs, land_cs, pack_v, land_v,
    line, plane, coarse, spread,
    load_sem, send_sem, recv_sem, line_send, line_recv, plane_send, plane_recv,
):
    nx, ny, nz = counts
    bx, by, bz = block
    px, py = bx + 2 * DEPTH, by + 2 * ROWS
    cx, cy, cz = bx // COARSE, by // COARSE, bz // COARSE
    ypad = line.shape[-2]
    mx, my, mz = lax.axis_index("gx"), lax.axis_index("gy"), lax.axis_index("gz")
    mine = (mx, my, mz)

    def present(offset):
        ok = None
        for here, step, size in zip(mine, offset, counts):
            if step == 0:
                continue
            good = here + step < size if step > 0 else here + step >= 0
            ok = good if ok is None else ok & good
        return ok

    def device(offset):
        return {
            "gx": mx + offset[0], "gy": my + offset[1], "gz": mz + offset[2]
        }

    offsets = [
        (dx, dy, dz)
        for dx in (-1, 0, 1) for dy in (-1, 0, 1) for dz in (-1, 0, 1)
        if (dx, dy, dz) != (0, 0, 0)
        and (dx == 0 or nx > 1) and (dy == 0 or ny > 1) and (dz == 0 or nz > 1)
    ]
    flat = [o for o in offsets if o[2] == 0]
    deep = [o for o in offsets if o[2] != 0]
    number = {o: i for i, o in enumerate(offsets)}

    cs[0] = jnp.zeros(cs.shape[1:], F32)
    loads = [
        pltpu.make_async_copy(
            ref, cs.at[0, f, pl.ds(DEPTH, bx), pl.ds(2 * ROWS, by)], load_sem.at[f]
        )
        for f, ref in ((0, c_ref), (1, s_ref))
    ]
    for load in loads:
        load.start()
    fresh[...] = jnp.zeros_like(fresh)
    land_cs[...] = jnp.zeros_like(land_cs)
    land_v[...] = jnp.zeros_like(land_v)

    barrier = pltpu.get_barrier_semaphore()
    total = jnp.int32(0)
    for o in offsets:
        ok = present(o)
        total = total + ok.astype(jnp.int32)

        @pl.when(ok)
        def _():
            pl.semaphore_signal(barrier, inc=1, device_id=device(o), device_id_type=MESH)

    for k in range(nz):
        far = jnp.abs(mz - k) >= 2
        total = total + far.astype(jnp.int32)

        @pl.when(far)
        def _():
            pl.semaphore_signal(
                barrier, inc=1, device_id={"gx": mx, "gy": my, "gz": k}, device_id_type=MESH
            )

    for i in range(nx):
        for j in range(ny):
            far = (jnp.abs(mx - i) >= 2) | (jnp.abs(my - j) >= 2)
            total = total + far.astype(jnp.int32)

            @pl.when(far)
            def _():
                pl.semaphore_signal(
                    barrier, inc=1, device_id={"gx": i, "gy": j, "gz": mz}, device_id_type=MESH
                )

    spread[...] = jnp.zeros_like(spread)
    for ref in (work_a, work_b, cs.at[1, 0]):
        lead = ref.shape[:-2]
        ref[..., 0:ROWS, :] = jnp.zeros(lead + (ROWS, LANES), F32)
        ref[..., ROWS + py:, :] = jnp.zeros(lead + (ROWS, LANES), F32)
    for load in loads:
        load.wait()
    pl.semaphore_wait(barrier, total)

    lane = lax.broadcasted_iota(jnp.int32, (py, LANES), 1)
    lane_by = lax.broadcasted_iota(jnp.int32, (by, LANES), 1)

    xs = {0: pl.ds(DEPTH, bx), 1: pl.ds(bx, DEPTH), -1: pl.ds(DEPTH, DEPTH)}
    xd = {0: pl.ds(DEPTH, bx), 1: pl.ds(0, DEPTH), -1: pl.ds(DEPTH + bx, DEPTH)}
    ys = {0: pl.ds(ROWS, by), 1: pl.ds(by, ROWS), -1: pl.ds(ROWS, ROWS)}
    yd = {0: pl.ds(ROWS, by), 1: pl.ds(0, ROWS), -1: pl.ds(ROWS + by, ROWS)}
    yp = {0: pl.ds(0, by), 1: pl.ds(by - ROWS, ROWS), -1: pl.ds(0, ROWS)}

    def copy(which, o, main, packed, landed):
        dx, dy, dz = o
        if dz == 0:
            base = 0 if which else ROWS
            source = main.at[:, xs[dx], pl.ds(ys[dy].start + base, ys[dy].size)]
            target = main.at[:, xd[dx], pl.ds(yd[dy].start + base, yd[dy].size)]
        else:
            side = 0 if dz > 0 else 1
            source = packed.at[side, :, yp[dy]]
            target = landed.at[dx + 1, side, :, yd[dy]]
        return pltpu.make_async_remote_copy(
            src_ref=source, dst_ref=target,
            send_sem=send_sem.at[which, number[o]], recv_sem=recv_sem.at[which, number[o]],
            device_id=device(o), device_id_type=MESH,
        )

    def send_flat(which, main, packed, landed):
        for o in flat:
            @pl.when(present(o))
            def _():
                copy(which, o, main, packed, landed).start()

    def send_deep(which, main, packed, landed):
        for f in range(packed.shape[1]):
            right = jnp.zeros((by, LANES), F32)
            left = jnp.zeros((by, LANES), F32)
            for j in range(bx):
                base = ROWS if which else 2 * ROWS
                v = main[f, DEPTH + j, base:base + by]
                here = lane_by // ROWS == j
                right = jnp.where(here, pltpu.roll(v, (ROWS * j + ROWS) % LANES, 1), right)
                left = jnp.where(here, pltpu.roll(v, (ROWS * j) % LANES, 1), left)
            packed[0, f] = right
            packed[1, f] = left
        for o in deep:
            @pl.when(present(o))
            def _():
                copy(which, o, main, packed, landed).start()

    def arrive(which, main, packed, landed):
        for o in flat + deep:
            @pl.when(present(tuple(-step for step in o)))
            def _():
                copy(which, o, main, packed, landed).wait_recv()

    def sent(which, main, packed, landed):
        for o in flat + deep:
            @pl.when(present(o))
            def _():
                copy(which, o, main, packed, landed).wait_send()

    def rim_of(landed, f, x):
        if x < DEPTH:
            slot, j = 2, bx - DEPTH + x
        elif x < DEPTH + bx:
            slot, j = 1, x - DEPTH
        else:
            slot, j = 0, x - DEPTH - bx
        before = pltpu.roll(landed[slot, 0, f], (LANES - ROWS - ROWS * j) % LANES, 1)
        after = pltpu.roll(landed[slot, 1, f], (LANES - ROWS * j) % LANES, 1)
        return jnp.where(
            lane < ROWS, after, jnp.where(lane >= LANES - ROWS, before, 0.0)
        )

    def line_copy(k, p):
        return pltpu.make_async_remote_copy(
            src_ref=line.at[k, mz], dst_ref=line.at[k, mz],
            send_sem=line_send.at[k, p], recv_sem=line_recv.at[k, mz],
            device_id={"gx": mx, "gy": my, "gz": p}, device_id_type=MESH,
        )

    def plane_copy(k, i, j):
        return pltpu.make_async_remote_copy(
            src_ref=plane.at[k, mx, my], dst_ref=plane.at[k, mx, my],
            send_sem=plane_send.at[k, i, j], recv_sem=plane_recv.at[k, mx, my],
            device_id={"gx": i, "gy": j, "gz": mz}, device_id_type=MESH,
        )

    def restrict_send(k, sums):
        row = lax.broadcasted_iota(jnp.int32, (ypad, LANES), 0)
        parts = []
        for a in range(cx):
            out = jnp.zeros((ypad, LANES), F32)
            for b in range(cy):
                t = jnp.sum(sums[a][b * COARSE:(b + 1) * COARSE], axis=0, keepdims=True)
                out = jnp.where(row == my * cy + b, t, out)
            parts.append(out)
        tall = jnp.concatenate(parts, axis=0)
        fine = lax.broadcasted_iota(jnp.int32, (bz, LANES), 0)
        cell = lax.broadcasted_iota(jnp.int32, (bz, LANES), 1)
        place = (cell == mz * cz + fine // COARSE).astype(F32)
        tall = jnp.dot(tall, place, preferred_element_type=F32, precision=HIGH)
        line[k, mz] = tall.reshape(cx, ypad, LANES)
        for p in range(nz):
            @pl.when(p != mz)
            def _():
                line_copy(k, p).start()

    def gather_middle(k):
        for p in range(nz):
            @pl.when(p != mz)
            def _():
                pltpu.make_async_remote_copy(
                    src_ref=line.at[k, p], dst_ref=line.at[k, p],
                    send_sem=line_send.at[k, p], recv_sem=line_recv.at[k, p],
                    device_id={"gx": mx, "gy": my, "gz": p}, device_id_type=MESH,
                ).wait_recv()
        acc = line[k, 0]
        for p in range(1, nz):
            acc = acc + line[k, p]
        plane[k, mx, my] = acc
        for i in range(nx):
            for j in range(ny):
                @pl.when((i != mx) | (j != my))
                def _():
                    plane_copy(k, i, j).start()

    def gather_end(k):
        for i in range(nx):
            for j in range(ny):
                @pl.when((i != mx) | (j != my))
                def _():
                    pltpu.make_async_remote_copy(
                        src_ref=plane.at[k, i, j], dst_ref=plane.at[k, i, j],
                        send_sem=plane_send.at[k, i, j], recv_sem=plane_recv.at[k, i, j],
                        device_id={"gx": i, "gy": j, "gz": mz}, device_id_type=MESH,
                    ).wait_recv()
        parts = []
        for i in range(nx):
            acc = plane[k, i, 0]
            for j in range(1, ny):
                acc = acc + plane[k, i, j]
            parts.append(acc)
        return jnp.concatenate(parts, axis=0)

    def gather_sent(k):
        for p in range(nz):
            @pl.when(p != mz)
            def _():
                line_copy(k, p).wait_send()
        for i in range(nx):
            for j in range(ny):
                @pl.when((i != mx) | (j != my))
                def _():
                    plane_copy(k, i, j).wait_send()

    body_rows = pl.ds(ROWS, py)

    def six(ref, x, size):
        planes = [[ref[p, x - 1 + i, body_rows] for i in range(size + 2)] for p in (0, 1)]
        out = []
        for i in range(1, size + 1):
            main, rim = planes[0][i], planes[1][i]
            m_up, m_down = pltpu.roll(main, 1, 1), pltpu.roll(main, LANES - 1, 1)
            r_up, r_down = pltpu.roll(rim, 1, 1), pltpu.roll(rim, LANES - 1, 1)
            first, last = lane == 0, lane == LANES - 1
            ends = (
                (jnp.where(first, r_up, m_up), jnp.where(last, r_down, m_down)),
                (jnp.where(first, m_up, r_up), jnp.where(last, m_down, r_down)),
            )
            for p in (0, 1):
                near = (
                    planes[p][i - 1], planes[p][i + 1],
                    ref[p, x - 1 + i, pl.ds(ROWS - 1, py)],
                    ref[p, x - 1 + i, pl.ds(ROWS + 1, py)],
                ) + ends[p]
                out.append((p, x - 1 + i, planes[p][i], near))
        return out

    def group_of(count):
        return max(g for g in range(1, 12) if count % g == 0)

    def sweep(source, target, margin):
        count = px - 2 * margin
        size = group_of(count)

        def step(g, carry):
            for part, x, v, near in six(source, margin + g * size, size):
                acc = (1.0 - OMEGA) * v + coef[6, part, x]
                for n in range(6):
                    acc = acc + coef[n, part, x] * near[n]
                target[part, x, body_rows] = acc
            return carry
        lax.fori_loop(0, count // size, step, 0)

    def core(source, x, weight):
        inner = pl.ds(2 * ROWS, by)
        own = pl.ds(ROWS, by)
        mid = source[0, x, inner]
        rim = source[1, x, inner]
        low = jnp.where(lane_by == 0, pltpu.roll(rim, 1, 1), pltpu.roll(mid, 1, 1))
        high = jnp.where(
            lane_by == LANES - 1, pltpu.roll(rim, LANES - 1, 1), pltpu.roll(mid, LANES - 1, 1)
        )
        near = (
            source[0, x - 1, inner], source[0, x + 1, inner],
            source[0, x, pl.ds(2 * ROWS - 1, by)], source[0, x, pl.ds(2 * ROWS + 1, by)],
            low, high,
        )
        acc = weight * mid + coef[6, 0, x, own]
        for n in range(6):
            acc = acc + coef[n, 0, x, own] * near[n]
        return acc

    both = cs.at[0]
    send_flat(0, both, pack_cs, land_cs)
    send_deep(0, both, pack_cs, land_cs)

    sums = []
    for a in range(cx):
        acc = jnp.zeros((by, LANES), F32)
        for t in range(COARSE):
            acc = acc + cs[0, 0, DEPTH + a * COARSE + t, 2 * ROWS:2 * ROWS + by]
        sums.append(acc * (1.0 / (COARSE * COARSE)))
    restrict_send(0, sums)
    gather_middle(0)
    arrive(0, both, pack_cs, land_cs)

    for f in range(2):
        for x in range(px):
            cs[1, f, x, body_rows] = rim_of(land_cs, f, x)

    size = group_of(px - 2)

    def make(g, carry):
        for part, x, c, near in six(cs.at[:, 0], 1 + g * size, size):
            faces = [0.5 * (c + n) for n in near]
            diag = (faces[0] + faces[1]) + (faces[2] + faces[3]) + (faces[4] + faces[5])
            here = c > 0.0
            w = jnp.where(here, OMEGA / jnp.where(here, diag, 1.0), 0.0)
            for n in range(6):
                coef[n, part, x] = w * faces[n]
            first = w * cs[part, 1, x, body_rows]
            coef[6, part, x] = first
            work_a[part, x, body_rows] = first
            if part == 0:
                scale[x] = (1.0 / OMEGA) * diag
        return carry
    lax.fori_loop(0, (px - 2) // size, make, 0)

    for cycle in range(CYCLES):
        if cycle == 0:
            order, first = [(work_a, work_b), (work_b, work_a), (work_a, work_b)], 2
        else:
            order, first = [(work_a, work_b), (work_b, work_a)] * 2, 1
        for i, (source, target) in enumerate(order):
            sweep(source, target, first + i)
        last = order[-1][1]
        which = 1 + 2 * cycle
        slot = which - 1
        main, packed, landed = fresh.at[slot], pack_v.at[slot], land_v.at[slot]
        fresh[slot, 0, DEPTH:DEPTH + bx, ROWS:ROWS + by] = (
            last[0, DEPTH:DEPTH + bx, 2 * ROWS:2 * ROWS + by]
        )

        sums = []
        for a in range(cx):
            acc = jnp.zeros((by, LANES), F32)
            for x in range(DEPTH + a * COARSE, DEPTH + a * COARSE + COARSE):
                acc = acc + core(last, x, -OMEGA) * scale[x, ROWS:ROWS + by]
            sums.append(acc)
        restrict_send(1 + cycle, sums)
        send_flat(which, main, packed, landed)
        send_deep(which, main, packed, landed)
        gather_middle(1 + cycle)

        if cycle == 0:
            cc = gather_end(0)
            shape = cc.shape
            row = lax.broadcasted_iota(jnp.int32, shape, 1)
            col = lax.broadcasted_iota(jnp.int32, shape, 2)
            blank = jnp.zeros((1,) + shape[1:], F32)

            def shifts(v):
                return (
                    jnp.concatenate([blank, v[:-1]], axis=0),
                    jnp.concatenate([v[1:], blank], axis=0),
                    jnp.where(row == 0, 0.0, pltpu.roll(v, 1, 1)),
                    jnp.where(row == shape[1] - 1, 0.0, pltpu.roll(v, shape[1] - 1, 1)),
                    jnp.where(col == 0, 0.0, pltpu.roll(v, 1, 2)),
                    jnp.where(col == LANES - 1, 0.0, pltpu.roll(v, LANES - 1, 2)),
                )

            faces = [0.5 * (cc + n) for n in shifts(cc)]
            diag = (faces[0] + faces[1]) + (faces[2] + faces[3]) + (faces[4] + faces[5])
            here = cc > 0.0
            w = jnp.where(here, OMEGA / jnp.where(here, diag, 1.0), 0.0)
            for n in range(6):
                coarse[n] = w * faces[n]
            coarse[6] = w

        rhs = gather_end(1 + cycle) * coarse[6]
        corr = rhs
        for _ in range(CSWEEPS - 1):
            acc = (1.0 - OMEGA) * corr + rhs
            for n, v in enumerate(shifts(corr)):
                acc = acc + coarse[n] * v
            corr = acc

        tall = corr.reshape(-1, LANES)
        cell = lax.broadcasted_iota(jnp.int32, (LANES, LANES), 0)
        fine = lax.broadcasted_iota(jnp.int32, (LANES, LANES), 1)
        to_main = (cell == mz * cz + fine // COARSE).astype(F32)
        to_rim = (
            ((fine < ROWS) & (cell == mz * cz + cz))
            | ((fine >= LANES - ROWS) & (cell == mz * cz - 1))
        ).astype(F32)
        for part, matrix in ((0, to_main), (1, to_rim)):
            wide = jnp.dot(tall, matrix, preferred_element_type=F32, precision=HIGH)
            spread[part, 1:1 + shape[0], ROWS:ROWS + shape[1]] = wide.reshape(shape)

        def lifted(part, x):
            a = mx * cx + 1 + (x - DEPTH) // COARSE
            rows = []
            for t in range(py // ROWS):
                one = spread[part, a, pl.ds(ROWS - 1 + my * cy + t, 1)]
                rows.append(jnp.broadcast_to(one, (ROWS, LANES)))
            return jnp.concatenate(rows, axis=0)

        lifts = {}
        for x in range(px):
            key = (x - DEPTH) // COARSE
            if key not in lifts:
                lifts[key] = (lifted(0, x), lifted(1, x))
        arrive(which, main, packed, landed)
        for x in range(px):
            key = (x - DEPTH) // COARSE
            work_a[0, x, body_rows] = fresh[slot, 0, x] + lifts[key][0]
            work_a[1, x, body_rows] = rim_of(land_v.at[slot], 0, x) + lifts[key][1]

        sweep(work_a, work_b, 1)
        sweep(work_b, work_a, 2)
        sweep(work_a, work_b, 3)
        if cycle == CYCLES - 1:
            for x in range(DEPTH, DEPTH + bx):
                o_ref[x - DEPTH] = core(work_b, x, 1.0 - OMEGA)
        else:
            which, slot = which + 1, slot + 1
            main, packed, landed = fresh.at[slot], pack_v.at[slot], land_v.at[slot]

            for x in range(DEPTH, DEPTH + bx):
                fresh[slot, 0, x, ROWS:ROWS + by] = core(work_b, x, 1.0 - OMEGA)
            send_flat(which, main, packed, landed)
            send_deep(which, main, packed, landed)
            arrive(which, main, packed, landed)
            for x in range(px):
                work_a[0, x, body_rows] = fresh[slot, 0, x]
                work_a[1, x, body_rows] = rim_of(land_v.at[slot], 0, x)

    sent(0, both, pack_cs, land_cs)
    for k in range(2 * CYCLES - 1):
        sent(1 + k, fresh.at[k], pack_v.at[k], land_v.at[k])
    for k in range(CYCLES + 1):
        gather_sent(k)


def body(counts, right_side, conductivity):
    nx, ny, nz = counts
    bx, by, bz = block = right_side.shape
    assert bz == LANES and bx * ROWS <= LANES and bx % COARSE == 0 and by % COARSE == 0
    assert nz * bz // COARSE <= LANES
    px, py = bx + 2 * DEPTH, by + 2 * ROWS
    cx = bx // COARSE
    ypad = -(-(ny * by // COARSE) // ROWS) * ROWS
    moves = 2 * CYCLES - 1
    vmem = pltpu.VMEM
    dma = pltpu.SemaphoreType.DMA
    return pl.pallas_call(
        functools.partial(kernel, counts, block),
        out_shape=jax.ShapeDtypeStruct(block, F32),
        in_specs=[pl.BlockSpec(memory_space=pltpu.HBM)] * 2,
        out_specs=pl.BlockSpec(memory_space=vmem),
        scratch_shapes=[
            vmem((2, 2, px, py + 2 * ROWS, LANES), F32),
            vmem((moves, 1, px, py, LANES), F32),
            vmem((2, px, py + 2 * ROWS, LANES), F32),
            vmem((2, px, py + 2 * ROWS, LANES), F32),
            vmem((7, 2, px, py, LANES), F32),
            vmem((px, py, LANES), F32),
            vmem((2, 2, by, LANES), F32),
            vmem((3, 2, 2, py, LANES), F32),
            vmem((moves, 2, 1, by, LANES), F32),
            vmem((moves, 3, 2, 1, py, LANES), F32),
            vmem((CYCLES + 1, nz, cx, ypad, LANES), F32),
            vmem((CYCLES + 1, nx, ny, cx, ypad, LANES), F32),
            vmem((7, nx * cx, ypad, LANES), F32),
            vmem((2, nx * cx + 2, ypad + 2 * ROWS, LANES), F32),
            dma((2,)),
            dma((moves + 1, 26)),
            dma((moves + 1, 26)),
            dma((CYCLES + 1, nz)),
            dma((CYCLES + 1, nz)),
            dma((CYCLES + 1, nx, ny)),
            dma((CYCLES + 1, nx, ny)),
        ],
        compiler_params=pltpu.CompilerParams(
            collective_id=0, has_side_effects=True, vmem_limit_bytes=40 * 1024 * 1024
        ),
    )(right_side, conductivity)


def solution(mesh):
    counts = tuple(mesh.shape[name] for name in ("gx", "gy", "gz"))
    return jax.shard_map(
        functools.partial(body, counts),
        mesh=mesh,
        in_specs=(P("gx", "gy", "gz"), P("gx", "gy", "gz")),
        out_specs=P("gx", "gy", "gz"),
        check_vma=False,
    )
```

```python
import functools

import jax
import jax.numpy as jnp
from jax import lax
from jax.experimental import pallas as pl
from jax.experimental.pallas import tpu as pltpu
from jax.sharding import PartitionSpec as P

COARSE = 8
SWEEPS = 4
CSWEEPS = 8
CYCLES = 2
OMEGA = 0.8
LANES = 128
ROWS = 8
DEPTH = SWEEPS + 1
MESH = pl.DeviceIdType.MESH
F32 = jnp.float32
HIGH = lax.Precision.HIGHEST


def kernel(
    counts, block, s_ref, c_ref, o_ref,
    cs, fresh, work_a, work_b, coef, scale, pack_cs, land_cs, pack_v, land_v,
    line, plane, coarse, spread,
    load_sem, send_sem, recv_sem, line_send, line_recv, plane_send, plane_recv,
):
    nx, ny, nz = counts
    bx, by, bz = block
    px, py = bx + 2 * DEPTH, by + 2 * ROWS
    cx, cy, cz = bx // COARSE, by // COARSE, bz // COARSE
    ypad = line.shape[-2]
    mx, my, mz = lax.axis_index("gx"), lax.axis_index("gy"), lax.axis_index("gz")
    mine = (mx, my, mz)

    def present(offset):
        ok = None
        for here, step, size in zip(mine, offset, counts):
            if step == 0:
                continue
            good = here + step < size if step > 0 else here + step >= 0
            ok = good if ok is None else ok & good
        return ok

    pair = nx == 2
    toward = 1 - 2 * mx
    steps_x = (0, 1) if pair else ((0, 1, -1) if nx > 1 else (0,))
    steps_y = (0, 1, -1) if ny > 1 else (0,)
    steps_z = (0, 1, -1) if nz > 1 else (0,)
    flat_groups = [(dy, 0) for dy in steps_y]
    deep_groups = [(dy, dz) for dz in steps_z if dz for dy in steps_y]
    number = {}
    for dy, dz in flat_groups + deep_groups:
        for dx in steps_x:
            if (dx, dy, dz) != (0, 0, 0):
                number[dx, dy, dz] = len(number)

    def device(offset):
        dx = toward if pair and offset[0] else offset[0]
        return {"gx": mx + dx, "gy": my + offset[1], "gz": mz + offset[2]}

    def each(groups, act, sign=1):
        for dy, dz in groups:
            def members():
                for dx in steps_x:
                    if (dx, dy, dz) not in number:
                        continue
                    if dx == 0 or pair:
                        act((dx, dy, dz))
                    else:
                        pl.when(present((sign * dx, 0, 0)))(lambda: act((dx, dy, dz)))
            if dy == 0 and dz == 0:
                members()
            else:
                pl.when(present((0, sign * dy, sign * dz)))(members)

    cs[0] = jnp.zeros(cs.shape[1:], F32)
    loads = [
        pltpu.make_async_copy(
            ref, cs.at[0, f, pl.ds(DEPTH, bx), pl.ds(2 * ROWS, by)], load_sem.at[f]
        )
        for f, ref in ((0, c_ref), (1, s_ref))
    ]
    for load in loads:
        load.start()
    fresh[...] = jnp.zeros_like(fresh)
    land_cs[...] = jnp.zeros_like(land_cs)
    land_v[...] = jnp.zeros_like(land_v)

    barrier = pltpu.get_barrier_semaphore()
    total = jnp.int32(0)
    for o in number:
        ok = present((0, o[1], o[2]) if pair else o)
        total = total + (1 if ok is None else ok.astype(jnp.int32))
    each(
        flat_groups + deep_groups,
        lambda o: pl.semaphore_signal(
            barrier, inc=1, device_id=device(o), device_id_type=MESH
        ),
    )

    for k in range(nz):
        far = jnp.abs(mz - k) >= 2
        total = total + far.astype(jnp.int32)

        @pl.when(far)
        def _():
            pl.semaphore_signal(
                barrier, inc=1, device_id={"gx": mx, "gy": my, "gz": k}, device_id_type=MESH
            )

    for i in range(nx):
        for j in range(ny):
            far = (jnp.abs(mx - i) >= 2) | (jnp.abs(my - j) >= 2)
            total = total + far.astype(jnp.int32)

            @pl.when(far)
            def _():
                pl.semaphore_signal(
                    barrier, inc=1, device_id={"gx": i, "gy": j, "gz": mz}, device_id_type=MESH
                )

    spread[...] = jnp.zeros_like(spread)
    for ref in (work_a, work_b, cs.at[1, 0]):
        lead = ref.shape[:-2]
        ref[..., 0:ROWS, :] = jnp.zeros(lead + (ROWS, LANES), F32)
        ref[..., ROWS + py:, :] = jnp.zeros(lead + (ROWS, LANES), F32)
    for load in loads:
        load.wait()
    pl.semaphore_wait(barrier, total)

    lane = lax.broadcasted_iota(jnp.int32, (py, LANES), 1)
    lane_by = lax.broadcasted_iota(jnp.int32, (by, LANES), 1)

    def x_ranges(dx, incoming):
        if dx == 0:
            return pl.ds(DEPTH, bx), pl.ds(DEPTH, bx), 1
        if pair:
            up = mx if incoming else 1 - mx
            return (
                pl.ds(DEPTH + (bx - DEPTH) * up, DEPTH),
                pl.ds((DEPTH + bx) * (1 - up), DEPTH), 2 * up,
            )
        if dx > 0:
            return pl.ds(bx, DEPTH), pl.ds(0, DEPTH), 2
        return pl.ds(DEPTH, DEPTH), pl.ds(DEPTH + bx, DEPTH), 0

    ys = {0: pl.ds(ROWS, by), 1: pl.ds(by, ROWS), -1: pl.ds(ROWS, ROWS)}
    yd = {0: pl.ds(ROWS, by), 1: pl.ds(0, ROWS), -1: pl.ds(ROWS + by, ROWS)}
    yp = {0: pl.ds(0, by), 1: pl.ds(by - ROWS, ROWS), -1: pl.ds(0, ROWS)}

    def copy(which, o, main, packed, landed, incoming=False):
        dx, dy, dz = o
        source_x, target_x, slot = x_ranges(dx, incoming)
        if dz == 0:
            base = 0 if which else ROWS
            source = main.at[:, source_x, pl.ds(ys[dy].start + base, ys[dy].size)]
            target = main.at[:, target_x, pl.ds(yd[dy].start + base, yd[dy].size)]
        else:
            side = 0 if dz > 0 else 1
            source = packed.at[side, :, yp[dy]]
            target = landed.at[slot, side, :, yd[dy]]
        return pltpu.make_async_remote_copy(
            src_ref=source, dst_ref=target,
            send_sem=send_sem.at[which, number[o]], recv_sem=recv_sem.at[which, number[o]],
            device_id=device(o), device_id_type=MESH,
        )

    def send_flat(which, main, packed, landed):
        each(flat_groups, lambda o: copy(which, o, main, packed, landed).start())

    def send_deep(which, main, packed, landed):
        for f in range(packed.shape[1]):
            right = jnp.zeros((by, LANES), F32)
            left = jnp.zeros((by, LANES), F32)
            for j in range(bx):
                base = ROWS if which else 2 * ROWS
                v = main[f, DEPTH + j, base:base + by]
                here = lane_by // ROWS == j
                right = jnp.where(here, pltpu.roll(v, (ROWS * j + ROWS) % LANES, 1), right)
                left = jnp.where(here, pltpu.roll(v, (ROWS * j) % LANES, 1), left)
            packed[0, f] = right
            packed[1, f] = left
        each(deep_groups, lambda o: copy(which, o, main, packed, landed).start())

    def arrive(which, main, packed, landed):
        each(
            flat_groups + deep_groups,
            lambda o: copy(which, o, main, packed, landed, True).wait_recv(), -1,
        )

    def sent(which, main, packed, landed):
        each(
            flat_groups + deep_groups,
            lambda o: copy(which, o, main, packed, landed).wait_send(),
        )

    def rim_of(landed, f, x):
        if x < DEPTH:
            slot, j = 2, bx - DEPTH + x
        elif x < DEPTH + bx:
            slot, j = 1, x - DEPTH
        else:
            slot, j = 0, x - DEPTH - bx
        before = pltpu.roll(landed[slot, 0, f], (LANES - ROWS - ROWS * j) % LANES, 1)
        after = pltpu.roll(landed[slot, 1, f], (LANES - ROWS * j) % LANES, 1)
        return jnp.where(
            lane < ROWS, after, jnp.where(lane >= LANES - ROWS, before, 0.0)
        )

    flat_me = mx * ny + my

    def others(me, size):
        for o in range(1, size):
            p = me + o
            yield jnp.where(p >= size, p - size, p)

    def line_copy(k, p, slot):
        return pltpu.make_async_remote_copy(
            src_ref=line.at[k, slot], dst_ref=line.at[k, slot],
            send_sem=line_send.at[k, p], recv_sem=line_recv.at[k, slot],
            device_id={"gx": mx, "gy": my, "gz": p}, device_id_type=MESH,
        )

    def plane_copy(k, q, slot):
        return pltpu.make_async_remote_copy(
            src_ref=plane.at[k, slot], dst_ref=plane.at[k, slot],
            send_sem=plane_send.at[k, q], recv_sem=plane_recv.at[k, slot],
            device_id={"gx": q // ny, "gy": q % ny, "gz": mz}, device_id_type=MESH,
        )

    def restrict_send(k, sums):
        row = lax.broadcasted_iota(jnp.int32, (ypad, LANES), 0)
        parts = []
        for a in range(cx):
            out = jnp.zeros((ypad, LANES), F32)
            for b in range(cy):
                t = jnp.sum(sums[a][b * COARSE:(b + 1) * COARSE], axis=0, keepdims=True)
                out = jnp.where(row == my * cy + b, t, out)
            parts.append(out)
        tall = jnp.concatenate(parts, axis=0)
        fine = lax.broadcasted_iota(jnp.int32, (bz, LANES), 0)
        cell = lax.broadcasted_iota(jnp.int32, (bz, LANES), 1)
        place = (cell == mz * cz + fine // COARSE).astype(F32)
        tall = jnp.dot(tall, place, preferred_element_type=F32, precision=HIGH)
        line[k, mz] = tall.reshape(cx, ypad, LANES)
        for p in others(mz, nz):
            line_copy(k, p, mz).start()

    def gather_middle(k):
        for p in others(mz, nz):
            line_copy(k, p, p).wait_recv()
        acc = line[k, 0]
        for p in range(1, nz):
            acc = acc + line[k, p]
        plane[k, flat_me] = acc
        for q in others(flat_me, nx * ny):
            plane_copy(k, q, flat_me).start()

    def gather_end(k):
        for q in others(flat_me, nx * ny):
            plane_copy(k, q, q).wait_recv()
        parts = []
        for i in range(nx):
            acc = plane[k, i * ny]
            for j in range(1, ny):
                acc = acc + plane[k, i * ny + j]
            parts.append(acc)
        return jnp.concatenate(parts, axis=0)

    def line_sent(k):
        for p in others(mz, nz):
            line_copy(k, p, mz).wait_send()

    def plane_sent(k):
        for q in others(flat_me, nx * ny):
            plane_copy(k, q, flat_me).wait_send()

    body_rows = pl.ds(ROWS, py)

    def six(ref, x, size):
        planes = [[ref[p, x - 1 + i, body_rows] for i in range(size + 2)] for p in (0, 1)]
        out = []
        for i in range(1, size + 1):
            main, rim = planes[0][i], planes[1][i]
            m_up, m_down = pltpu.roll(main, 1, 1), pltpu.roll(main, LANES - 1, 1)
            r_up, r_down = pltpu.roll(rim, 1, 1), pltpu.roll(rim, LANES - 1, 1)
            first, last = lane == 0, lane == LANES - 1
            ends = (
                (jnp.where(first, r_up, m_up), jnp.where(last, r_down, m_down)),
                (jnp.where(first, m_up, r_up), jnp.where(last, m_down, r_down)),
            )
            for p in (0, 1):
                near = (
                    planes[p][i - 1], planes[p][i + 1],
                    ref[p, x - 1 + i, pl.ds(ROWS - 1, py)],
                    ref[p, x - 1 + i, pl.ds(ROWS + 1, py)],
                ) + ends[p]
                out.append((p, x - 1 + i, planes[p][i], near))
        return out

    def group_of(count):
        return max(g for g in range(1, 12) if count % g == 0)

    def sweep(source, target, margin):
        count = px - 2 * margin
        size = group_of(count)

        def step(g, carry):
            for part, x, v, near in six(source, margin + g * size, size):
                acc = (1.0 - OMEGA) * v + coef[6, part, x]
                for n in range(6):
                    acc = acc + coef[n, part, x] * near[n]
                target[part, x, body_rows] = acc
            return carry
        lax.fori_loop(0, count // size, step, 0)

    def core(source, x, weight):
        inner = pl.ds(2 * ROWS, by)
        own = pl.ds(ROWS, by)
        mid = source[0, x, inner]
        rim = source[1, x, inner]
        low = jnp.where(lane_by == 0, pltpu.roll(rim, 1, 1), pltpu.roll(mid, 1, 1))
        high = jnp.where(
            lane_by == LANES - 1, pltpu.roll(rim, LANES - 1, 1), pltpu.roll(mid, LANES - 1, 1)
        )
        near = (
            source[0, x - 1, inner], source[0, x + 1, inner],
            source[0, x, pl.ds(2 * ROWS - 1, by)], source[0, x, pl.ds(2 * ROWS + 1, by)],
            low, high,
        )
        acc = weight * mid + coef[6, 0, x, own]
        for n in range(6):
            acc = acc + coef[n, 0, x, own] * near[n]
        return acc

    both = cs.at[0]
    send_flat(0, both, pack_cs, land_cs)
    send_deep(0, both, pack_cs, land_cs)

    sums = []
    for a in range(cx):
        acc = jnp.zeros((by, LANES), F32)
        for t in range(COARSE):
            acc = acc + cs[0, 0, DEPTH + a * COARSE + t, 2 * ROWS:2 * ROWS + by]
        sums.append(acc * (1.0 / (COARSE * COARSE)))
    restrict_send(0, sums)
    gather_middle(0)
    arrive(0, both, pack_cs, land_cs)

    for f in range(2):
        for x in range(px):
            cs[1, f, x, body_rows] = rim_of(land_cs, f, x)

    size = group_of(px - 2)

    def make(g, carry):
        for part, x, c, near in six(cs.at[:, 0], 1 + g * size, size):
            faces = [0.5 * (c + n) for n in near]
            diag = (faces[0] + faces[1]) + (faces[2] + faces[3]) + (faces[4] + faces[5])
            here = c > 0.0
            w = jnp.where(here, OMEGA / jnp.where(here, diag, 1.0), 0.0)
            for n in range(6):
                coef[n, part, x] = w * faces[n]
            first = w * cs[part, 1, x, body_rows]
            coef[6, part, x] = first
            work_a[part, x, body_rows] = first
            if part == 0:
                scale[x] = (1.0 / OMEGA) * diag
        return carry
    lax.fori_loop(0, (px - 2) // size, make, 0)

    for cycle in range(CYCLES):
        if cycle == 0:
            order, first = [(work_a, work_b), (work_b, work_a), (work_a, work_b)], 2
        else:
            order, first = [(work_a, work_b), (work_b, work_a)] * 2, 1
        for i, (source, target) in enumerate(order):
            sweep(source, target, first + i)
        last = order[-1][1]
        which = 1 + 2 * cycle
        slot = which - 1
        main, packed, landed = fresh.at[slot], pack_v.at[slot], land_v.at[slot]
        fresh[slot, 0, DEPTH:DEPTH + bx, ROWS:ROWS + by] = (
            last[0, DEPTH:DEPTH + bx, 2 * ROWS:2 * ROWS + by]
        )

        sums = []
        for a in range(cx):
            acc = jnp.zeros((by, LANES), F32)
            for x in range(DEPTH + a * COARSE, DEPTH + a * COARSE + COARSE):
                acc = acc + core(last, x, -OMEGA) * scale[x, ROWS:ROWS + by]
            sums.append(acc)
        restrict_send(1 + cycle, sums)
        send_flat(which, main, packed, landed)
        send_deep(which, main, packed, landed)
        gather_middle(1 + cycle)

        line_sent(1 + cycle)
        if cycle == 0:
            sent(0, both, pack_cs, land_cs)
            line_sent(0)
            plane_sent(0)
        else:
            plane_sent(cycle)
        sent(which, main, packed, landed)
        arrive(which, main, packed, landed)
        for x in range(px):
            work_a[1, x, body_rows] = rim_of(land_v.at[slot], 0, x)

        if cycle == 0:
            cc = gather_end(0)
            shape = cc.shape
            row = lax.broadcasted_iota(jnp.int32, shape, 1)
            col = lax.broadcasted_iota(jnp.int32, shape, 2)
            blank = jnp.zeros((1,) + shape[1:], F32)

            def shifts(v):
                return (
                    jnp.concatenate([blank, v[:-1]], axis=0),
                    jnp.concatenate([v[1:], blank], axis=0),
                    jnp.where(row == 0, 0.0, pltpu.roll(v, 1, 1)),
                    jnp.where(row == shape[1] - 1, 0.0, pltpu.roll(v, shape[1] - 1, 1)),
                    jnp.where(col == 0, 0.0, pltpu.roll(v, 1, 2)),
                    jnp.where(col == LANES - 1, 0.0, pltpu.roll(v, LANES - 1, 2)),
                )

            faces = [0.5 * (cc + n) for n in shifts(cc)]
            diag = (faces[0] + faces[1]) + (faces[2] + faces[3]) + (faces[4] + faces[5])
            here = cc > 0.0
            w = jnp.where(here, OMEGA / jnp.where(here, diag, 1.0), 0.0)
            for n in range(6):
                coarse[n] = w * faces[n]
            coarse[6] = w

        rhs = gather_end(1 + cycle) * coarse[6]
        corr = rhs
        for _ in range(CSWEEPS - 1):
            acc = (1.0 - OMEGA) * corr + rhs
            for n, v in enumerate(shifts(corr)):
                acc = acc + coarse[n] * v
            corr = acc

        tall = corr.reshape(-1, LANES)
        cell = lax.broadcasted_iota(jnp.int32, (LANES, LANES), 0)
        fine = lax.broadcasted_iota(jnp.int32, (LANES, LANES), 1)
        to_main = (cell == mz * cz + fine // COARSE).astype(F32)
        to_rim = (
            ((fine < ROWS) & (cell == mz * cz + cz))
            | ((fine >= LANES - ROWS) & (cell == mz * cz - 1))
        ).astype(F32)
        for part, matrix in ((0, to_main), (1, to_rim)):
            wide = jnp.dot(tall, matrix, preferred_element_type=F32, precision=HIGH)
            spread[part, 1:1 + shape[0], ROWS:ROWS + shape[1]] = wide.reshape(shape)

        def lifted(part, x):
            a = mx * cx + 1 + (x - DEPTH) // COARSE
            rows = []
            for t in range(py // ROWS):
                one = spread[part, a, pl.ds(ROWS - 1 + my * cy + t, 1)]
                rows.append(jnp.broadcast_to(one, (ROWS, LANES)))
            return jnp.concatenate(rows, axis=0)

        lifts = {}
        for x in range(px):
            key = (x - DEPTH) // COARSE
            if key not in lifts:
                lifts[key] = (lifted(0, x), lifted(1, x))
        for x in range(px):
            key = (x - DEPTH) // COARSE
            work_a[0, x, body_rows] = fresh[slot, 0, x] + lifts[key][0]
            work_a[1, x, body_rows] = work_a[1, x, body_rows] + lifts[key][1]

        sweep(work_a, work_b, 1)
        sweep(work_b, work_a, 2)
        sweep(work_a, work_b, 3)
        if cycle == CYCLES - 1:
            for x in range(DEPTH, DEPTH + bx):
                o_ref[x - DEPTH] = core(work_b, x, 1.0 - OMEGA)
        else:
            which, slot = which + 1, slot + 1
            main, packed, landed = fresh.at[slot], pack_v.at[slot], land_v.at[slot]

            for x in range(DEPTH, DEPTH + bx):
                fresh[slot, 0, x, ROWS:ROWS + by] = core(work_b, x, 1.0 - OMEGA)
            send_flat(which, main, packed, landed)
            send_deep(which, main, packed, landed)
            sent(which, main, packed, landed)
            arrive(which, main, packed, landed)
            for x in range(px):
                work_a[0, x, body_rows] = fresh[slot, 0, x]
                work_a[1, x, body_rows] = rim_of(land_v.at[slot], 0, x)

    plane_sent(CYCLES)


def body(counts, right_side, conductivity):
    nx, ny, nz = counts
    bx, by, bz = block = right_side.shape
    assert bz == LANES and bx * ROWS <= LANES and bx % COARSE == 0 and by % COARSE == 0
    assert nz * bz // COARSE <= LANES
    px, py = bx + 2 * DEPTH, by + 2 * ROWS
    cx = bx // COARSE
    ypad = -(-(ny * by // COARSE) // ROWS) * ROWS
    moves = 2 * CYCLES - 1
    vmem = pltpu.VMEM
    dma = pltpu.SemaphoreType.DMA
    return pl.pallas_call(
        functools.partial(kernel, counts, block),
        out_shape=jax.ShapeDtypeStruct(block, F32),
        in_specs=[pl.BlockSpec(memory_space=pltpu.HBM)] * 2,
        out_specs=pl.BlockSpec(memory_space=vmem),
        scratch_shapes=[
            vmem((2, 2, px, py + 2 * ROWS, LANES), F32),
            vmem((moves, 1, px, py, LANES), F32),
            vmem((2, px, py + 2 * ROWS, LANES), F32),
            vmem((2, px, py + 2 * ROWS, LANES), F32),
            vmem((7, 2, px, py, LANES), F32),
            vmem((px, py, LANES), F32),
            vmem((2, 2, by, LANES), F32),
            vmem((3, 2, 2, py, LANES), F32),
            vmem((moves, 2, 1, by, LANES), F32),
            vmem((moves, 3, 2, 1, py, LANES), F32),
            vmem((CYCLES + 1, nz, cx, ypad, LANES), F32),
            vmem((CYCLES + 1, nx * ny, cx, ypad, LANES), F32),
            vmem((7, nx * cx, ypad, LANES), F32),
            vmem((2, nx * cx + 2, ypad + 2 * ROWS, LANES), F32),
            dma((2,)),
            dma((moves + 1, 26)),
            dma((moves + 1, 26)),
            dma((CYCLES + 1, nz)),
            dma((CYCLES + 1, nz)),
            dma((CYCLES + 1, nx * ny)),
            dma((CYCLES + 1, nx * ny)),
        ],
        compiler_params=pltpu.CompilerParams(
            collective_id=0, has_side_effects=True, vmem_limit_bytes=60 * 1024 * 1024
        ),
    )(right_side, conductivity)


def solution(mesh):
    counts = tuple(mesh.shape[name] for name in ("gx", "gy", "gz"))
    return jax.shard_map(
        functools.partial(body, counts),
        mesh=mesh,
        in_specs=(P("gx", "gy", "gz"), P("gx", "gy", "gz")),
        out_specs=P("gx", "gy", "gz"),
        check_vma=False,
    )
```

```python
import functools

import jax
import jax.numpy as jnp
from jax import lax
from jax.experimental import pallas as pl
from jax.experimental.pallas import tpu as pltpu
from jax.sharding import PartitionSpec as P

COARSE = 8
SWEEPS = 4
CSWEEPS = 8
CYCLES = 2
OMEGA = 0.8
LANES = 128
ROWS = 8
DEPTH = SWEEPS + 1
MESH = pl.DeviceIdType.MESH
F32 = jnp.float32
HIGH = lax.Precision.HIGHEST


def kernel(
    counts, block, s_ref, c_ref, o_ref,
    cs, fresh, work_a, work_b, rim_a, rim_b, coef, rim_coef, scale, pack_cs, land_cs, pack_v, land_v,
    line, plane, coarse, spread,
    load_sem, send_sem, recv_sem, line_send, line_recv, plane_send, plane_recv,
):
    nx, ny, nz = counts
    bx, by, bz = block
    px, py = bx + 2 * DEPTH, by + 2 * ROWS
    cx, cy, cz = bx // COARSE, by // COARSE, bz // COARSE
    ypad = line.shape[-2]
    mx, my, mz = lax.axis_index("gx"), lax.axis_index("gy"), lax.axis_index("gz")
    mine = (mx, my, mz)

    def present(offset):
        ok = None
        for here, step, size in zip(mine, offset, counts):
            if step == 0:
                continue
            good = here + step < size if step > 0 else here + step >= 0
            ok = good if ok is None else ok & good
        return ok

    pair = nx == 2
    toward = 1 - 2 * mx
    steps_x = (0, 1) if pair else ((0, 1, -1) if nx > 1 else (0,))
    steps_y = (0, 1, -1) if ny > 1 else (0,)
    steps_z = (0, 1, -1) if nz > 1 else (0,)
    flat_groups = [(dy, 0) for dy in steps_y]
    deep_groups = [(dy, dz) for dz in steps_z if dz for dy in steps_y]
    number = {}
    for dy, dz in flat_groups + deep_groups:
        for dx in steps_x:
            if (dx, dy, dz) != (0, 0, 0):
                number[dx, dy, dz] = len(number)

    def device(offset):
        dx = toward if pair and offset[0] else offset[0]
        return {"gx": mx + dx, "gy": my + offset[1], "gz": mz + offset[2]}

    def each(groups, act, sign=1):
        for dy, dz in groups:
            def members():
                for dx in steps_x:
                    if (dx, dy, dz) not in number:
                        continue
                    if dx == 0 or pair:
                        act((dx, dy, dz))
                    else:
                        pl.when(present((sign * dx, 0, 0)))(lambda: act((dx, dy, dz)))
            if dy == 0 and dz == 0:
                members()
            else:
                pl.when(present((0, sign * dy, sign * dz)))(members)

    cs[...] = jnp.zeros_like(cs)
    loads = [
        pltpu.make_async_copy(
            ref, cs.at[f, pl.ds(DEPTH, bx), pl.ds(2 * ROWS, by)], load_sem.at[f]
        )
        for f, ref in ((0, c_ref), (1, s_ref))
    ]
    for load in loads:
        load.start()
    fresh[...] = jnp.zeros_like(fresh)
    land_cs[...] = jnp.zeros_like(land_cs)
    land_v[...] = jnp.zeros_like(land_v)

    barrier = pltpu.get_barrier_semaphore()
    total = jnp.int32(0)
    for o in number:
        ok = present((0, o[1], o[2]) if pair else o)
        total = total + (1 if ok is None else ok.astype(jnp.int32))
    each(
        flat_groups + deep_groups,
        lambda o: pl.semaphore_signal(
            barrier, inc=1, device_id=device(o), device_id_type=MESH
        ),
    )

    for k in range(nz):
        far = jnp.abs(mz - k) >= 2
        total = total + far.astype(jnp.int32)

        @pl.when(far)
        def _():
            pl.semaphore_signal(
                barrier, inc=1, device_id={"gx": mx, "gy": my, "gz": k}, device_id_type=MESH
            )

    for i in range(nx):
        for j in range(ny):
            far = (jnp.abs(mx - i) >= 2) | (jnp.abs(my - j) >= 2)
            total = total + far.astype(jnp.int32)

            @pl.when(far)
            def _():
                pl.semaphore_signal(
                    barrier, inc=1, device_id={"gx": i, "gy": j, "gz": mz}, device_id_type=MESH
                )

    spread[...] = jnp.zeros_like(spread)
    for ref in (work_a, work_b, rim_a, rim_b):
        lead = ref.shape[:-2]
        ref[..., 0:ROWS, :] = jnp.zeros(lead + (ROWS, LANES), F32)
        ref[..., ROWS + py:, :] = jnp.zeros(lead + (ROWS, LANES), F32)
    for load in loads:
        load.wait()
    pl.semaphore_wait(barrier, total)

    lane = lax.broadcasted_iota(jnp.int32, (py, LANES), 1)
    lane_by = lax.broadcasted_iota(jnp.int32, (by, LANES), 1)

    def x_ranges(dx, incoming):
        if dx == 0:
            return pl.ds(DEPTH, bx), pl.ds(DEPTH, bx), 1
        if pair:
            up = mx if incoming else 1 - mx
            return (
                pl.ds(DEPTH + (bx - DEPTH) * up, DEPTH),
                pl.ds((DEPTH + bx) * (1 - up), DEPTH), 2 * (1 - up),
            )
        if dx > 0:
            return pl.ds(bx, DEPTH), pl.ds(0, DEPTH), 0
        return pl.ds(DEPTH, DEPTH), pl.ds(DEPTH + bx, DEPTH), 2

    ys = {0: pl.ds(2 * ROWS, by), 1: pl.ds(ROWS + by, ROWS), -1: pl.ds(2 * ROWS, ROWS)}
    yd = {0: pl.ds(2 * ROWS, by), 1: pl.ds(ROWS, ROWS), -1: pl.ds(2 * ROWS + by, ROWS)}
    yp = {0: pl.ds(0, by), 1: pl.ds(by - ROWS, ROWS), -1: pl.ds(0, ROWS)}

    def copy(which, o, main, packed, landed, incoming=False):
        dx, dy, dz = o
        source_x, target_x, slot = x_ranges(dx, incoming)
        if dz == 0:
            source = main.at[:, source_x, ys[dy]]
            target = main.at[:, target_x, yd[dy]]
        else:
            side = 0 if dz > 0 else 1
            source = packed.at[side, :, yp[dy]]
            target = landed.at[slot, side, :, yd[dy]]
        return pltpu.make_async_remote_copy(
            src_ref=source, dst_ref=target,
            send_sem=send_sem.at[which, number[o]], recv_sem=recv_sem.at[which, number[o]],
            device_id=device(o), device_id_type=MESH,
        )

    def send_flat(which, main, packed, landed):
        each(flat_groups, lambda o: copy(which, o, main, packed, landed).start())

    def send_deep(which, main, packed, landed):
        for f in range(packed.shape[1]):
            right = jnp.zeros((by, LANES), F32)
            left = jnp.zeros((by, LANES), F32)
            for j in range(bx):
                v = main[f, DEPTH + j, 2 * ROWS:2 * ROWS + by]
                here = lane_by // ROWS == j
                right = jnp.where(here, pltpu.roll(v, (ROWS * j + ROWS) % LANES, 1), right)
                left = jnp.where(here, pltpu.roll(v, (ROWS * j) % LANES, 1), left)
            packed[0, f] = right
            packed[1, f] = left
        each(deep_groups, lambda o: copy(which, o, main, packed, landed).start())

    def arrive(which, main, packed, landed):
        each(
            flat_groups + deep_groups,
            lambda o: copy(which, o, main, packed, landed, True).wait_recv(), -1,
        )

    def sent(which, main, packed, landed):
        each(
            flat_groups + deep_groups,
            lambda o: copy(which, o, main, packed, landed).wait_send(),
        )

    flat_me = mx * ny + my

    def others(me, size):
        for o in range(1, size):
            p = me + o
            yield jnp.where(p >= size, p - size, p)

    def line_copy(k, p, slot):
        return pltpu.make_async_remote_copy(
            src_ref=line.at[k, slot], dst_ref=line.at[k, slot],
            send_sem=line_send.at[k, p], recv_sem=line_recv.at[k, slot],
            device_id={"gx": mx, "gy": my, "gz": p}, device_id_type=MESH,
        )

    def plane_copy(k, q, slot):
        return pltpu.make_async_remote_copy(
            src_ref=plane.at[k, slot], dst_ref=plane.at[k, slot],
            send_sem=plane_send.at[k, q], recv_sem=plane_recv.at[k, slot],
            device_id={"gx": q // ny, "gy": q % ny, "gz": mz}, device_id_type=MESH,
        )

    def restrict_send(k, sums):
        row = lax.broadcasted_iota(jnp.int32, (ypad, LANES), 0)
        parts = []
        for a in range(cx):
            out = jnp.zeros((ypad, LANES), F32)
            for b in range(cy):
                t = jnp.sum(sums[a][b * COARSE:(b + 1) * COARSE], axis=0, keepdims=True)
                out = jnp.where(row == my * cy + b, t, out)
            parts.append(out)
        tall = jnp.concatenate(parts, axis=0)
        fine = lax.broadcasted_iota(jnp.int32, (bz, LANES), 0)
        cell = lax.broadcasted_iota(jnp.int32, (bz, LANES), 1)
        place = (cell == mz * cz + fine // COARSE).astype(F32)
        tall = jnp.dot(tall, place, preferred_element_type=F32, precision=HIGH)
        line[k, mz] = tall.reshape(cx, ypad, LANES)
        for p in others(mz, nz):
            line_copy(k, p, mz).start()

    def gather_middle(k):
        for p in others(mz, nz):
            line_copy(k, p, p).wait_recv()
        acc = line[k, 0]
        for p in range(1, nz):
            acc = acc + line[k, p]
        plane[k, flat_me] = acc
        for q in others(flat_me, nx * ny):
            plane_copy(k, q, flat_me).start()

    def gather_end(k):
        for q in others(flat_me, nx * ny):
            plane_copy(k, q, q).wait_recv()
        parts = []
        for i in range(nx):
            acc = plane[k, i * ny]
            for j in range(1, ny):
                acc = acc + plane[k, i * ny + j]
            parts.append(acc)
        return jnp.concatenate(parts, axis=0)

    def line_sent(k):
        for p in others(mz, nz):
            line_copy(k, p, mz).wait_send()

    def plane_sent(k):
        for q in others(flat_me, nx * ny):
            plane_copy(k, q, flat_me).wait_send()

    body_rows = pl.ds(ROWS, py)
    own_rows = pl.ds(2 * ROWS, by)
    sides = [(slot, side) for slot in range(3) for side in range(2)]

    def lanes(rows):
        return lax.broadcasted_iota(jnp.int32, (rows.size, LANES), 1)

    def place_of(x):
        if x < DEPTH:
            return 0, bx - DEPTH + x
        if x < DEPTH + bx:
            return 1, x - DEPTH
        return 2, x - DEPTH - bx

    def ends_of(rim, rows):
        last = lanes(rows) % ROWS == ROWS - 1
        return [
            jnp.where(last, rim[slot, 0, rows], pltpu.roll(rim[slot, 1, rows], ROWS - 2, 1))
            for slot in range(3)
        ]

    def near_main(main, ends, x, rows):
        lane = lanes(rows)
        slot, j = place_of(x)
        v = main[x, rows]
        up, down = pltpu.roll(v, 1, 1), pltpu.roll(v, LANES - 1, 1)
        end = pltpu.roll(ends[slot], (2 * LANES - ROWS * j - ROWS + 1) % LANES, 1)
        return v, up, (
            main[x - 1, rows], main[x + 1, rows],
            main[x, pl.ds(rows.start - 1, rows.size)], main[x, pl.ds(rows.start + 1, rows.size)],
            jnp.where(lane == 0, end, up), jnp.where(lane == LANES - 1, end, down),
        )

    def collect(tips, x, up):
        slot, j = place_of(x)
        turned = pltpu.roll(up, ROWS * j, 1) if j else up
        tips[slot] = jnp.where(lane // ROWS == j, turned, tips[slot])

    def near_rim(rim, tips, slot, side):
        rows = body_rows
        q = rim[slot, side, rows]
        zero = jnp.zeros((py, LANES), F32)
        before = pltpu.roll(rim[slot - 1, side, rows], ROWS, 1) if slot > 0 else zero
        after = pltpu.roll(rim[slot + 1, side, rows], LANES - ROWS, 1) if slot < 2 else zero
        low, high = pltpu.roll(q, 1, 1), pltpu.roll(q, LANES - 1, 1)
        if side == 0:
            high = jnp.where(
                lane % ROWS == ROWS - 1, pltpu.roll(tips[slot], ROWS - 2, 1), high
            )
        else:
            low = jnp.where(lane % ROWS == 0, tips[slot], low)
        return q, (
            jnp.where(lane < ROWS, before, pltpu.roll(q, ROWS, 1)),
            jnp.where(lane >= LANES - ROWS, after, pltpu.roll(q, LANES - ROWS, 1)),
            rim[slot, side, pl.ds(ROWS - 1, py)], rim[slot, side, pl.ds(ROWS + 1, py)],
            low, high,
        )

    def no_tips():
        return [jnp.zeros((py, LANES), F32) for _ in range(3)]

    def sweep(source, target, margin):
        main, rim = source
        ends, tips = ends_of(rim, body_rows), no_tips()
        for x in range(margin, px - margin):
            v, up, near = near_main(main, ends, x, body_rows)
            collect(tips, x, up)
            acc = (1.0 - OMEGA) * v + coef[6, x]
            for n in range(6):
                acc = acc + coef[n, x] * near[n]
            target[0][x, body_rows] = acc
        for slot, side in sides:
            q, near = near_rim(rim, tips, slot, side)
            acc = (1.0 - OMEGA) * q + rim_coef[6, slot, side]
            for n in range(6):
                acc = acc + rim_coef[n, slot, side] * near[n]
            target[1][slot, side, body_rows] = acc

    def core(source, x, ends, weight):
        v, _, near = near_main(source[0], ends, x, own_rows)
        own = pl.ds(ROWS, by)
        acc = weight * v + coef[6, x, own]
        for n in range(6):
            acc = acc + coef[n, x, own] * near[n]
        return acc

    both = cs
    send_flat(0, both, pack_cs, land_cs)
    send_deep(0, both, pack_cs, land_cs)

    sums = []
    for a in range(cx):
        acc = jnp.zeros((by, LANES), F32)
        for t in range(COARSE):
            acc = acc + cs[0, DEPTH + a * COARSE + t, 2 * ROWS:2 * ROWS + by]
        sums.append(acc * (1.0 / (COARSE * COARSE)))
    restrict_send(0, sums)
    gather_middle(0)
    arrive(0, both, pack_cs, land_cs)

    def weights(c, near):
        faces = [0.5 * (c + n) for n in near]
        diag = (faces[0] + faces[1]) + (faces[2] + faces[3]) + (faces[4] + faces[5])
        here = c > 0.0
        w = jnp.where(here, OMEGA / jnp.where(here, diag, 1.0), 0.0)
        return faces, diag, w

    rim_c = land_cs.at[:, :, 0]
    ends, tips = ends_of(rim_c, body_rows), no_tips()
    for x in range(1, px - 1):
        c, up, near = near_main(cs.at[0], ends, x, body_rows)
        collect(tips, x, up)
        faces, diag, w = weights(c, near)
        for n in range(6):
            coef[n, x] = w * faces[n]
        first = w * cs[1, x, body_rows]
        coef[6, x] = first
        work_a[x, body_rows] = first
        scale[x] = (1.0 / OMEGA) * diag
    for slot, side in sides:
        c, near = near_rim(rim_c, tips, slot, side)
        faces, diag, w = weights(c, near)
        for n in range(6):
            rim_coef[n, slot, side] = w * faces[n]
        first = w * land_cs[slot, side, 1, body_rows]
        rim_coef[6, slot, side] = first
        rim_a[slot, side, body_rows] = first

    field_a, field_b = (work_a, rim_a), (work_b, rim_b)
    for cycle in range(CYCLES):
        if cycle == 0:
            order, first = [(field_a, field_b), (field_b, field_a), (field_a, field_b)], 2
        else:
            order = [(start, field_b), (field_b, field_a), (field_a, field_b), (field_b, field_a)]
            first = 1
        for i, (source, target) in enumerate(order):
            sweep(source, target, first + i)
        last = order[-1][1]
        which = 1 + 2 * cycle
        slot = which - 1
        main, packed, landed = fresh.at[slot], pack_v.at[slot], land_v.at[slot]
        fresh[slot, 0, DEPTH:DEPTH + bx, 2 * ROWS:2 * ROWS + by] = (
            last[0][DEPTH:DEPTH + bx, 2 * ROWS:2 * ROWS + by]
        )

        sums = []
        ends = ends_of(last[1], own_rows)
        for a in range(cx):
            acc = jnp.zeros((by, LANES), F32)
            for x in range(DEPTH + a * COARSE, DEPTH + a * COARSE + COARSE):
                acc = acc + core(last, x, ends, -OMEGA) * scale[x, ROWS:ROWS + by]
            sums.append(acc)
        restrict_send(1 + cycle, sums)
        send_flat(which, main, packed, landed)
        send_deep(which, main, packed, landed)
        gather_middle(1 + cycle)

        line_sent(1 + cycle)
        if cycle == 0:
            sent(0, both, pack_cs, land_cs)
            line_sent(0)
            plane_sent(0)
        else:
            plane_sent(cycle)
        sent(which, main, packed, landed)
        arrive(which, main, packed, landed)

        if cycle == 0:
            cc = gather_end(0)
            shape = cc.shape
            row = lax.broadcasted_iota(jnp.int32, shape, 1)
            col = lax.broadcasted_iota(jnp.int32, shape, 2)
            blank = jnp.zeros((1,) + shape[1:], F32)

            def shifts(v):
                return (
                    jnp.concatenate([blank, v[:-1]], axis=0),
                    jnp.concatenate([v[1:], blank], axis=0),
                    jnp.where(row == 0, 0.0, pltpu.roll(v, 1, 1)),
                    jnp.where(row == shape[1] - 1, 0.0, pltpu.roll(v, shape[1] - 1, 1)),
                    jnp.where(col == 0, 0.0, pltpu.roll(v, 1, 2)),
                    jnp.where(col == LANES - 1, 0.0, pltpu.roll(v, LANES - 1, 2)),
                )

            faces = [0.5 * (cc + n) for n in shifts(cc)]
            diag = (faces[0] + faces[1]) + (faces[2] + faces[3]) + (faces[4] + faces[5])
            here = cc > 0.0
            w = jnp.where(here, OMEGA / jnp.where(here, diag, 1.0), 0.0)
            for n in range(6):
                coarse[n] = w * faces[n]
            coarse[6] = w

        rhs = gather_end(1 + cycle) * coarse[6]
        corr = rhs
        for _ in range(CSWEEPS - 1):
            acc = (1.0 - OMEGA) * corr + rhs
            for n, v in enumerate(shifts(corr)):
                acc = acc + coarse[n] * v
            corr = acc

        tall = corr.reshape(-1, LANES)
        cell = lax.broadcasted_iota(jnp.int32, (LANES, LANES), 0)
        fine = lax.broadcasted_iota(jnp.int32, (LANES, LANES), 1)
        to_main = (cell == mz * cz + fine // COARSE).astype(F32)
        to_left = (cell == mz * cz - 1).astype(F32)
        to_right = (cell == mz * cz + cz).astype(F32)
        for part, matrix in enumerate((to_main, to_left, to_right)):
            wide = jnp.dot(tall, matrix, preferred_element_type=F32, precision=HIGH)
            spread[part, 1:1 + shape[0], ROWS:ROWS + shape[1]] = wide.reshape(shape)

        def lifted(part, a):
            rows = []
            for t in range(py // ROWS):
                one = spread[part, mx * cx + 1 + a, pl.ds(ROWS - 1 + my * cy + t, 1)]
                rows.append(jnp.broadcast_to(one, (ROWS, LANES)))
            return jnp.concatenate(rows, axis=0)

        lifts = [lifted(0, a) for a in range(-1, cx + 1)]
        for x in range(px):
            work_a[x, body_rows] = (
                fresh[slot, 0, x, body_rows] + lifts[(x - DEPTH) // COARSE + 1]
            )
        for side in range(2):
            own = lifted(1 + side, 0)
            for a in range(1, cx):
                own = jnp.where(lane // (COARSE * ROWS) == a, lifted(1 + side, a), own)
            for k, lift in enumerate((lifted(1 + side, -1), own, lifted(1 + side, cx))):
                rim_a[k, side, body_rows] = land_v[slot, k, side, 0, body_rows] + lift

        sweep(field_a, field_b, 1)
        sweep(field_b, field_a, 2)
        sweep(field_a, field_b, 3)
        ends = ends_of(rim_b, own_rows)
        if cycle == CYCLES - 1:
            for x in range(DEPTH, DEPTH + bx):
                o_ref[x - DEPTH] = core(field_b, x, ends, 1.0 - OMEGA)
        else:
            which, slot = which + 1, slot + 1
            main, packed, landed = fresh.at[slot], pack_v.at[slot], land_v.at[slot]
            for x in range(DEPTH, DEPTH + bx):
                fresh[slot, 0, x, 2 * ROWS:2 * ROWS + by] = core(field_b, x, ends, 1.0 - OMEGA)
            send_flat(which, main, packed, landed)
            send_deep(which, main, packed, landed)
            sent(which, main, packed, landed)
            arrive(which, main, packed, landed)
            start = (fresh.at[slot, 0], land_v.at[slot, :, :, 0])

    plane_sent(CYCLES)


def body(counts, right_side, conductivity):
    nx, ny, nz = counts
    bx, by, bz = block = right_side.shape
    assert bz == LANES and bx * ROWS == LANES and COARSE == ROWS and bx % COARSE == 0 and by % COARSE == 0
    assert nz * bz // COARSE <= LANES
    px, py = bx + 2 * DEPTH, by + 2 * ROWS
    tall = py + 2 * ROWS
    cx = bx // COARSE
    ypad = -(-(ny * by // COARSE) // ROWS) * ROWS
    moves = 2 * CYCLES - 1
    vmem = pltpu.VMEM
    dma = pltpu.SemaphoreType.DMA
    return pl.pallas_call(
        functools.partial(kernel, counts, block),
        out_shape=jax.ShapeDtypeStruct(block, F32),
        in_specs=[pl.BlockSpec(memory_space=pltpu.HBM)] * 2,
        out_specs=pl.BlockSpec(memory_space=vmem),
        scratch_shapes=[
            vmem((2, px, tall, LANES), F32),
            vmem((moves, 1, px, tall, LANES), F32),
            vmem((px, tall, LANES), F32),
            vmem((px, tall, LANES), F32),
            vmem((3, 2, tall, LANES), F32),
            vmem((3, 2, tall, LANES), F32),
            vmem((7, px, py, LANES), F32),
            vmem((7, 3, 2, py, LANES), F32),
            vmem((px, py, LANES), F32),
            vmem((2, 2, by, LANES), F32),
            vmem((3, 2, 2, tall, LANES), F32),
            vmem((moves, 2, 1, by, LANES), F32),
            vmem((moves, 3, 2, 1, tall, LANES), F32),
            vmem((CYCLES + 1, nz, cx, ypad, LANES), F32),
            vmem((CYCLES + 1, nx * ny, cx, ypad, LANES), F32),
            vmem((7, nx * cx, ypad, LANES), F32),
            vmem((3, nx * cx + 2, ypad + 2 * ROWS, LANES), F32),
            dma((2,)),
            dma((moves + 1, 26)),
            dma((moves + 1, 26)),
            dma((CYCLES + 1, nz)),
            dma((CYCLES + 1, nz)),
            dma((CYCLES + 1, nx * ny)),
            dma((CYCLES + 1, nx * ny)),
        ],
        compiler_params=pltpu.CompilerParams(
            collective_id=0, has_side_effects=True, vmem_limit_bytes=60 * 1024 * 1024
        ),
    )(right_side, conductivity)


def solution(mesh):
    counts = tuple(mesh.shape[name] for name in ("gx", "gy", "gz"))
    return jax.shard_map(
        functools.partial(body, counts),
        mesh=mesh,
        in_specs=(P("gx", "gy", "gz"), P("gx", "gy", "gz")),
        out_specs=P("gx", "gy", "gz"),
        check_vma=False,
    )
```

```python
import functools

import jax
import jax.numpy as jnp
from jax import lax
from jax.experimental import pallas as pl
from jax.experimental.pallas import tpu as pltpu
from jax.sharding import PartitionSpec as P

COARSE = 8
SWEEPS = 4
CSWEEPS = 8
CYCLES = 2
OMEGA = 0.8
LANES = 128
ROWS = 8
DEPTH = SWEEPS + 1
MESH = pl.DeviceIdType.MESH
F32 = jnp.float32
HIGH = lax.Precision.HIGHEST


def kernel(
    counts, block, s_ref, c_ref, o_ref,
    cs, fresh, work_a, work_b, rim_a, rim_b, coef, rim_coef, scale, pack_cs, land_cs, pack_v, land_v,
    line, plane, coarse, spread,
    load_sem, send_sem, recv_sem, line_send, line_recv, plane_send, plane_recv,
):
    nx, ny, nz = counts
    bx, by, bz = block
    px, py = bx + 2 * DEPTH, by + 2 * ROWS
    cx, cy, cz = bx // COARSE, by // COARSE, bz // COARSE
    ypad = line.shape[-2]
    mx, my, mz = lax.axis_index("gx"), lax.axis_index("gy"), lax.axis_index("gz")
    mine = (mx, my, mz)

    def present(offset):
        ok = None
        for here, step, size in zip(mine, offset, counts):
            if step == 0:
                continue
            good = here + step < size if step > 0 else here + step >= 0
            ok = good if ok is None else ok & good
        return ok

    pair = nx == 2
    toward = 1 - 2 * mx
    steps_x = (0, 1) if pair else ((0, 1, -1) if nx > 1 else (0,))
    steps_y = (0, 1, -1) if ny > 1 else (0,)
    steps_z = (0, 1, -1) if nz > 1 else (0,)
    flat_groups = [(dy, 0) for dy in steps_y]
    deep_groups = [(dy, dz) for dz in steps_z if dz for dy in steps_y]
    number = {}
    for dy, dz in flat_groups + deep_groups:
        for dx in steps_x:
            if (dx, dy, dz) != (0, 0, 0):
                number[dx, dy, dz] = len(number)

    def device(offset):
        dx = toward if pair and offset[0] else offset[0]
        return {"gx": mx + dx, "gy": my + offset[1], "gz": mz + offset[2]}

    def each(groups, act, sign=1):
        for dy, dz in groups:
            def members():
                for dx in steps_x:
                    if (dx, dy, dz) not in number:
                        continue
                    if dx == 0 or pair:
                        act((dx, dy, dz))
                    else:
                        pl.when(present((sign * dx, 0, 0)))(lambda: act((dx, dy, dz)))
            if dy == 0 and dz == 0:
                members()
            else:
                pl.when(present((0, sign * dy, sign * dz)))(members)

    cs[...] = jnp.zeros_like(cs)
    loads = [
        pltpu.make_async_copy(
            ref, cs.at[f, pl.ds(DEPTH, bx), pl.ds(2 * ROWS, by)], load_sem.at[f]
        )
        for f, ref in ((0, c_ref), (1, s_ref))
    ]
    for load in loads:
        load.start()
    fresh[...] = jnp.zeros_like(fresh)
    land_cs[...] = jnp.zeros_like(land_cs)
    land_v[...] = jnp.zeros_like(land_v)

    barrier = pltpu.get_barrier_semaphore()
    total = jnp.int32(0)
    for o in number:
        ok = present((0, o[1], o[2]) if pair else o)
        total = total + (1 if ok is None else ok.astype(jnp.int32))
    each(
        flat_groups + deep_groups,
        lambda o: pl.semaphore_signal(
            barrier, inc=1, device_id=device(o), device_id_type=MESH
        ),
    )

    for k in range(nz):
        far = jnp.abs(mz - k) >= 2
        total = total + far.astype(jnp.int32)

        @pl.when(far)
        def _():
            pl.semaphore_signal(
                barrier, inc=1, device_id={"gx": mx, "gy": my, "gz": k}, device_id_type=MESH
            )

    for i in range(nx):
        for j in range(ny):
            far = (jnp.abs(mx - i) >= 2) | (jnp.abs(my - j) >= 2)
            total = total + far.astype(jnp.int32)

            @pl.when(far)
            def _():
                pl.semaphore_signal(
                    barrier, inc=1, device_id={"gx": i, "gy": j, "gz": mz}, device_id_type=MESH
                )

    spread[...] = jnp.zeros_like(spread)
    work_a[...] = jnp.zeros_like(work_a)
    for x in (0, px - 1):
        work_b[x] = jnp.zeros(work_b.shape[1:], F32)
    rim_a[...] = jnp.zeros_like(rim_a)
    for ref in (work_b, rim_b):
        lead = ref.shape[:-2]
        ref[..., 0:ROWS, :] = jnp.zeros(lead + (ROWS, LANES), F32)
        ref[..., ROWS + py:, :] = jnp.zeros(lead + (ROWS, LANES), F32)
    for load in loads:
        load.wait()
    pl.semaphore_wait(barrier, total)

    lane = lax.broadcasted_iota(jnp.int32, (py, LANES), 1)
    lane_by = lax.broadcasted_iota(jnp.int32, (by, LANES), 1)

    def x_ranges(dx, incoming):
        if dx == 0:
            return pl.ds(DEPTH, bx), pl.ds(DEPTH, bx), 1
        if pair:
            up = mx if incoming else 1 - mx
            return (
                pl.ds(DEPTH + (bx - DEPTH) * up, DEPTH),
                pl.ds((DEPTH + bx) * (1 - up), DEPTH), 2 * (1 - up),
            )
        if dx > 0:
            return pl.ds(bx, DEPTH), pl.ds(0, DEPTH), 0
        return pl.ds(DEPTH, DEPTH), pl.ds(DEPTH + bx, DEPTH), 2

    ys = {0: pl.ds(2 * ROWS, by), 1: pl.ds(ROWS + by, ROWS), -1: pl.ds(2 * ROWS, ROWS)}
    yd = {0: pl.ds(2 * ROWS, by), 1: pl.ds(ROWS, ROWS), -1: pl.ds(2 * ROWS + by, ROWS)}
    yp = {0: pl.ds(0, by), 1: pl.ds(by - ROWS, ROWS), -1: pl.ds(0, ROWS)}

    def copy(which, o, main, packed, landed, incoming=False):
        dx, dy, dz = o
        source_x, target_x, slot = x_ranges(dx, incoming)
        if dz == 0:
            source = main.at[:, source_x, ys[dy]]
            target = main.at[:, target_x, yd[dy]]
        else:
            side = 0 if dz > 0 else 1
            source = packed.at[side, :, yp[dy]]
            target = landed.at[slot, side, :, yd[dy]]
        return pltpu.make_async_remote_copy(
            src_ref=source, dst_ref=target,
            send_sem=send_sem.at[which, number[o]], recv_sem=recv_sem.at[which, number[o]],
            device_id=device(o), device_id_type=MESH,
        )

    def send_flat(which, main, packed, landed):
        each(flat_groups, lambda o: copy(which, o, main, packed, landed).start())

    def send_deep(which, main, packed, landed):
        for f in range(packed.shape[1]):
            right = jnp.zeros((by, LANES), F32)
            left = jnp.zeros((by, LANES), F32)
            for j in range(bx):
                v = main[f, DEPTH + j, 2 * ROWS:2 * ROWS + by]
                here = lane_by // ROWS == j
                right = jnp.where(here, pltpu.roll(v, (ROWS * j + ROWS) % LANES, 1), right)
                left = jnp.where(here, pltpu.roll(v, (ROWS * j) % LANES, 1), left)
            packed[0, f] = right
            packed[1, f] = left
        each(deep_groups, lambda o: copy(which, o, main, packed, landed).start())

    def arrive(which, main, packed, landed):
        each(
            flat_groups + deep_groups,
            lambda o: copy(which, o, main, packed, landed, True).wait_recv(), -1,
        )

    def sent(which, main, packed, landed):
        each(
            flat_groups + deep_groups,
            lambda o: copy(which, o, main, packed, landed).wait_send(),
        )

    flat_me = mx * ny + my

    def others(me, size):
        for o in range(1, size):
            p = me + o
            yield jnp.where(p >= size, p - size, p)

    def line_copy(k, p, slot):
        return pltpu.make_async_remote_copy(
            src_ref=line.at[k, slot], dst_ref=line.at[k, slot],
            send_sem=line_send.at[k, p], recv_sem=line_recv.at[k, slot],
            device_id={"gx": mx, "gy": my, "gz": p}, device_id_type=MESH,
        )

    def plane_copy(k, q, slot):
        return pltpu.make_async_remote_copy(
            src_ref=plane.at[k, slot], dst_ref=plane.at[k, slot],
            send_sem=plane_send.at[k, q], recv_sem=plane_recv.at[k, slot],
            device_id={"gx": q // ny, "gy": q % ny, "gz": mz}, device_id_type=MESH,
        )

    def restrict_send(k, sums):
        row = lax.broadcasted_iota(jnp.int32, (ypad, LANES), 0)
        parts = []
        for a in range(cx):
            out = jnp.zeros((ypad, LANES), F32)
            for b in range(cy):
                t = jnp.sum(sums[a][b * COARSE:(b + 1) * COARSE], axis=0, keepdims=True)
                out = jnp.where(row == my * cy + b, t, out)
            parts.append(out)
        tall = jnp.concatenate(parts, axis=0)
        fine = lax.broadcasted_iota(jnp.int32, (bz, LANES), 0)
        cell = lax.broadcasted_iota(jnp.int32, (bz, LANES), 1)
        place = (cell == mz * cz + fine // COARSE).astype(F32)
        tall = jnp.dot(tall, place, preferred_element_type=F32, precision=HIGH)
        line[k, mz] = tall.reshape(cx, ypad, LANES)
        for p in others(mz, nz):
            line_copy(k, p, mz).start()

    def gather_middle(k):
        for p in others(mz, nz):
            line_copy(k, p, p).wait_recv()
        acc = line[k, 0]
        for p in range(1, nz):
            acc = acc + line[k, p]
        plane[k, flat_me] = acc
        for q in others(flat_me, nx * ny):
            plane_copy(k, q, flat_me).start()

    def gather_end(k):
        for q in others(flat_me, nx * ny):
            plane_copy(k, q, q).wait_recv()
        parts = []
        for i in range(nx):
            acc = plane[k, i * ny]
            for j in range(1, ny):
                acc = acc + plane[k, i * ny + j]
            parts.append(acc)
        return jnp.concatenate(parts, axis=0)

    def line_sent(k):
        for p in others(mz, nz):
            line_copy(k, p, mz).wait_send()

    def plane_sent(k):
        for q in others(flat_me, nx * ny):
            plane_copy(k, q, flat_me).wait_send()

    body_rows = pl.ds(ROWS, py)
    own_rows = pl.ds(2 * ROWS, by)
    sides = [(slot, side) for slot in range(3) for side in range(2)]

    def lanes(rows):
        return lax.broadcasted_iota(jnp.int32, (rows.size, LANES), 1)

    def place_of(x):
        if x < DEPTH:
            return 0, bx - DEPTH + x
        if x < DEPTH + bx:
            return 1, x - DEPTH
        return 2, x - DEPTH - bx

    def ends_of(rim, rows):
        last = lanes(rows) % ROWS == ROWS - 1
        return [
            jnp.where(last, rim[slot, 0, rows], pltpu.roll(rim[slot, 1, rows], ROWS - 2, 1))
            for slot in range(3)
        ]

    def near_main(main, ends, x, rows):
        lane = lanes(rows)
        slot, j = place_of(x)
        v = main[x, rows]
        up, down = pltpu.roll(v, 1, 1), pltpu.roll(v, LANES - 1, 1)
        end = pltpu.roll(ends[slot], (2 * LANES - ROWS * j - ROWS + 1) % LANES, 1)
        return v, up, (
            main[x - 1, rows], main[x + 1, rows],
            main[x, pl.ds(rows.start - 1, rows.size)], main[x, pl.ds(rows.start + 1, rows.size)],
            jnp.where(lane == 0, end, up), jnp.where(lane == LANES - 1, end, down),
        )

    def collect(tips, x, up):
        slot, j = place_of(x)
        turned = pltpu.roll(up, ROWS * j, 1) if j else up
        tips[slot] = jnp.where(lane // ROWS == j, turned, tips[slot])

    def near_rim(rim, tips, slot, side):
        rows = body_rows
        q = rim[slot, side, rows]
        zero = jnp.zeros((py, LANES), F32)
        before = pltpu.roll(rim[slot - 1, side, rows], ROWS, 1) if slot > 0 else zero
        after = pltpu.roll(rim[slot + 1, side, rows], LANES - ROWS, 1) if slot < 2 else zero
        low, high = pltpu.roll(q, 1, 1), pltpu.roll(q, LANES - 1, 1)
        if side == 0:
            high = jnp.where(
                lane % ROWS == ROWS - 1, pltpu.roll(tips[slot], ROWS - 2, 1), high
            )
        else:
            low = jnp.where(lane % ROWS == 0, tips[slot], low)
        return q, (
            jnp.where(lane < ROWS, before, pltpu.roll(q, ROWS, 1)),
            jnp.where(lane >= LANES - ROWS, after, pltpu.roll(q, LANES - ROWS, 1)),
            rim[slot, side, pl.ds(ROWS - 1, py)], rim[slot, side, pl.ds(ROWS + 1, py)],
            low, high,
        )

    def no_tips():
        return [jnp.zeros((py, LANES), F32) for _ in range(3)]

    def sweep(source, target, margin):
        main, rim = source
        ends, tips = ends_of(rim, body_rows), no_tips()
        for x in range(margin, px - margin):
            v, up, near = near_main(main, ends, x, body_rows)
            collect(tips, x, up)
            acc = (1.0 - OMEGA) * v + coef[6, x]
            for n in range(6):
                acc = acc + coef[n, x] * near[n]
            target[0][x, body_rows] = acc
        for slot, side in sides:
            q, near = near_rim(rim, tips, slot, side)
            acc = (1.0 - OMEGA) * q + rim_coef[6, slot, side]
            for n in range(6):
                acc = acc + rim_coef[n, slot, side] * near[n]
            target[1][slot, side, body_rows] = acc

    def core(source, x, ends, weight):
        v, _, near = near_main(source[0], ends, x, own_rows)
        own = pl.ds(ROWS, by)
        acc = weight * v + coef[6, x, own]
        for n in range(6):
            acc = acc + coef[n, x, own] * near[n]
        return acc

    both = cs
    send_flat(0, both, pack_cs, land_cs)
    send_deep(0, both, pack_cs, land_cs)

    sums = []
    for a in range(cx):
        acc = jnp.zeros((by, LANES), F32)
        for t in range(COARSE):
            acc = acc + cs[0, DEPTH + a * COARSE + t, 2 * ROWS:2 * ROWS + by]
        sums.append(acc * (1.0 / (COARSE * COARSE)))
    restrict_send(0, sums)
    gather_middle(0)
    arrive(0, both, pack_cs, land_cs)

    def weights(c, near):
        faces = [0.5 * (c + n) for n in near]
        diag = (faces[0] + faces[1]) + (faces[2] + faces[3]) + (faces[4] + faces[5])
        here = c > 0.0
        w = jnp.where(here, OMEGA / jnp.where(here, diag, 1.0), 0.0)
        return faces, diag, w

    rim_c = land_cs.at[:, :, 0]
    ends, tips = ends_of(rim_c, body_rows), no_tips()
    for x in range(1, px - 1):
        c, up, near = near_main(cs.at[0], ends, x, body_rows)
        collect(tips, x, up)
        faces, diag, w = weights(c, near)
        for n in range(6):
            coef[n, x] = w * faces[n]
        first = w * cs[1, x, body_rows]
        coef[6, x] = first
        scale[x] = (1.0 / OMEGA) * diag
    for slot, side in sides:
        c, near = near_rim(rim_c, tips, slot, side)
        faces, diag, w = weights(c, near)
        for n in range(6):
            rim_coef[n, slot, side] = w * faces[n]
        first = w * land_cs[slot, side, 1, body_rows]
        rim_coef[6, slot, side] = first

    cc = gather_end(0)
    shape = cc.shape
    row = lax.broadcasted_iota(jnp.int32, shape, 1)
    col = lax.broadcasted_iota(jnp.int32, shape, 2)
    blank = jnp.zeros((1,) + shape[1:], F32)

    def shifts(v):
        return (
            jnp.concatenate([blank, v[:-1]], axis=0),
            jnp.concatenate([v[1:], blank], axis=0),
            jnp.where(row == 0, 0.0, pltpu.roll(v, 1, 1)),
            jnp.where(row == shape[1] - 1, 0.0, pltpu.roll(v, shape[1] - 1, 1)),
            jnp.where(col == 0, 0.0, pltpu.roll(v, 1, 2)),
            jnp.where(col == LANES - 1, 0.0, pltpu.roll(v, LANES - 1, 2)),
        )

    faces = [0.5 * (cc + n) for n in shifts(cc)]
    diag = (faces[0] + faces[1]) + (faces[2] + faces[3]) + (faces[4] + faces[5])
    here = cc > 0.0
    w = jnp.where(here, OMEGA / jnp.where(here, diag, 1.0), 0.0)
    for n in range(6):
        coarse[n] = w * faces[n]
    coarse[6] = w

    sent(0, both, pack_cs, land_cs)
    line_sent(0)

    field_a, field_b = (work_a, rim_a), (work_b, rim_b)

    def sweeps():
        def two(_, carry):
            sweep(field_a, field_b, 1)
            sweep(field_b, field_a, 1)
            return carry
        lax.fori_loop(0, SWEEPS // 2, two, 0)

    def one_cycle(cycle, carry):
        sweeps()
        last = field_a
        which = 1 + 2 * cycle
        slot = which - 1
        main, packed, landed = fresh.at[slot], pack_v.at[slot], land_v.at[slot]
        fresh[slot, 0, DEPTH:DEPTH + bx, 2 * ROWS:2 * ROWS + by] = (
            last[0][DEPTH:DEPTH + bx, 2 * ROWS:2 * ROWS + by]
        )

        sums = []
        ends = ends_of(last[1], own_rows)
        for a in range(cx):
            acc = jnp.zeros((by, LANES), F32)
            for x in range(DEPTH + a * COARSE, DEPTH + a * COARSE + COARSE):
                acc = acc + core(last, x, ends, -OMEGA) * scale[x, ROWS:ROWS + by]
            sums.append(acc)
        restrict_send(1 + cycle, sums)
        send_flat(which, main, packed, landed)
        send_deep(which, main, packed, landed)
        gather_middle(1 + cycle)

        line_sent(1 + cycle)
        plane_sent(cycle)
        sent(which, main, packed, landed)
        arrive(which, main, packed, landed)

        rhs = gather_end(1 + cycle) * coarse[6]
        corr = rhs
        for _ in range(CSWEEPS - 1):
            acc = (1.0 - OMEGA) * corr + rhs
            for n, v in enumerate(shifts(corr)):
                acc = acc + coarse[n] * v
            corr = acc

        tall = corr.reshape(-1, LANES)
        cell = lax.broadcasted_iota(jnp.int32, (LANES, LANES), 0)
        fine = lax.broadcasted_iota(jnp.int32, (LANES, LANES), 1)
        to_main = (cell == mz * cz + fine // COARSE).astype(F32)
        to_left = (cell == mz * cz - 1).astype(F32)
        to_right = (cell == mz * cz + cz).astype(F32)
        for part, matrix in enumerate((to_main, to_left, to_right)):
            wide = jnp.dot(tall, matrix, preferred_element_type=F32, precision=HIGH)
            spread[part, 1:1 + shape[0], ROWS:ROWS + shape[1]] = wide.reshape(shape)

        def lifted(part, a):
            rows = []
            for t in range(py // ROWS):
                one = spread[part, mx * cx + 1 + a, pl.ds(ROWS - 1 + my * cy + t, 1)]
                rows.append(jnp.broadcast_to(one, (ROWS, LANES)))
            return jnp.concatenate(rows, axis=0)

        lifts = [lifted(0, a) for a in range(-1, cx + 1)]
        for x in range(px):
            work_a[x, body_rows] = (
                fresh[slot, 0, x, body_rows] + lifts[(x - DEPTH) // COARSE + 1]
            )
        for side in range(2):
            own = lifted(1 + side, 0)
            for a in range(1, cx):
                own = jnp.where(lane // (COARSE * ROWS) == a, lifted(1 + side, a), own)
            for k, lift in enumerate((lifted(1 + side, -1), own, lifted(1 + side, cx))):
                rim_a[k, side, body_rows] = land_v[slot, k, side, 0, body_rows] + lift

        sweeps()

        @pl.when(cycle < CYCLES - 1)
        def _():
            inner = (pl.ds(DEPTH, bx), own_rows)
            main, packed, landed = fresh.at[slot + 1], pack_v.at[slot + 1], land_v.at[slot + 1]
            fresh[slot + 1, 0, *inner] = work_a[inner]
            send_flat(which + 1, main, packed, landed)
            send_deep(which + 1, main, packed, landed)
            sent(which + 1, main, packed, landed)
            arrive(which + 1, main, packed, landed)
            work_a[:, body_rows] = fresh[slot + 1, 0, :, body_rows]
            for k, side in sides:
                rim_a[k, side, body_rows] = land_v[slot + 1, k, side, 0, body_rows]

        return carry
    lax.fori_loop(0, CYCLES, one_cycle, 0)
    o_ref[...] = work_a[pl.ds(DEPTH, bx), own_rows]
    plane_sent(CYCLES)


def body(counts, right_side, conductivity):
    nx, ny, nz = counts
    bx, by, bz = block = right_side.shape
    assert bz == LANES and bx * ROWS == LANES and COARSE == ROWS and bx % COARSE == 0 and by % COARSE == 0
    assert nz * bz // COARSE <= LANES
    px, py = bx + 2 * DEPTH, by + 2 * ROWS
    tall = py + 2 * ROWS
    cx = bx // COARSE
    ypad = -(-(ny * by // COARSE) // ROWS) * ROWS
    moves = 2 * CYCLES - 1
    vmem = pltpu.VMEM
    dma = pltpu.SemaphoreType.DMA
    return pl.pallas_call(
        functools.partial(kernel, counts, block),
        out_shape=jax.ShapeDtypeStruct(block, F32),
        in_specs=[pl.BlockSpec(memory_space=pltpu.HBM)] * 2,
        out_specs=pl.BlockSpec(memory_space=vmem),
        scratch_shapes=[
            vmem((2, px, tall, LANES), F32),
            vmem((moves, 1, px, tall, LANES), F32),
            vmem((px, tall, LANES), F32),
            vmem((px, tall, LANES), F32),
            vmem((3, 2, tall, LANES), F32),
            vmem((3, 2, tall, LANES), F32),
            vmem((7, px, py, LANES), F32),
            vmem((7, 3, 2, py, LANES), F32),
            vmem((px, py, LANES), F32),
            vmem((2, 2, by, LANES), F32),
            vmem((3, 2, 2, tall, LANES), F32),
            vmem((moves, 2, 1, by, LANES), F32),
            vmem((moves, 3, 2, 1, tall, LANES), F32),
            vmem((CYCLES + 1, nz, cx, ypad, LANES), F32),
            vmem((CYCLES + 1, nx * ny, cx, ypad, LANES), F32),
            vmem((7, nx * cx, ypad, LANES), F32),
            vmem((3, nx * cx + 2, ypad + 2 * ROWS, LANES), F32),
            dma((2,)),
            dma((moves + 1, 26)),
            dma((moves + 1, 26)),
            dma((CYCLES + 1, nz)),
            dma((CYCLES + 1, nz)),
            dma((CYCLES + 1, nx * ny)),
            dma((CYCLES + 1, nx * ny)),
        ],
        compiler_params=pltpu.CompilerParams(
            collective_id=0, has_side_effects=True, vmem_limit_bytes=60 * 1024 * 1024
        ),
    )(right_side, conductivity)


def solution(mesh):
    counts = tuple(mesh.shape[name] for name in ("gx", "gy", "gz"))
    return jax.shard_map(
        functools.partial(body, counts),
        mesh=mesh,
        in_specs=(P("gx", "gy", "gz"), P("gx", "gy", "gz")),
        out_specs=P("gx", "gy", "gz"),
        check_vma=False,
    )
```

```python
import functools

import jax
import jax.numpy as jnp
from jax import lax
from jax.experimental import pallas as pl
from jax.experimental.pallas import tpu as pltpu
from jax.sharding import PartitionSpec as P

COARSE = 8
SWEEPS = 4
CSWEEPS = 8
CYCLES = 2
OMEGA = 0.8
LANES = 128
ROWS = 8
DEPTH = SWEEPS + 1
MESH = pl.DeviceIdType.MESH
F32 = jnp.float32
HIGH = lax.Precision.HIGHEST


def kernel(
    counts, block, s_ref, c_ref, o_ref,
    cs, fresh, work_a, work_b, coef, scale, pack_cs, land_cs, pack_v, land_v,
    line, plane, coarse, spread,
    load_sem, send_sem, recv_sem, line_send, line_recv, plane_send, plane_recv,
):
    nx, ny, nz = counts
    bx, by, bz = block
    px, py = bx + 2 * DEPTH, by + 2 * ROWS
    cx, cy, cz = bx // COARSE, by // COARSE, bz // COARSE
    ypad = line.shape[-2]
    mx, my, mz = lax.axis_index("gx"), lax.axis_index("gy"), lax.axis_index("gz")
    mine = (mx, my, mz)

    def present(offset):
        ok = None
        for here, step, size in zip(mine, offset, counts):
            if step == 0:
                continue
            good = here + step < size if step > 0 else here + step >= 0
            ok = good if ok is None else ok & good
        return ok

    pair = nx == 2
    toward = 1 - 2 * mx
    steps_x = (0, 1) if pair else ((0, 1, -1) if nx > 1 else (0,))
    steps_y = (0, 1, -1) if ny > 1 else (0,)
    steps_z = (0, 1, -1) if nz > 1 else (0,)
    flat_groups = [(dy, 0) for dy in steps_y]
    deep_groups = [(dy, dz) for dz in steps_z if dz for dy in steps_y]
    number = {}
    for dy, dz in flat_groups + deep_groups:
        for dx in steps_x:
            if (dx, dy, dz) != (0, 0, 0):
                number[dx, dy, dz] = len(number)

    def device(offset):
        dx = toward if pair and offset[0] else offset[0]
        return {"gx": mx + dx, "gy": my + offset[1], "gz": mz + offset[2]}

    def each(groups, act, sign=1):
        for dy, dz in groups:
            def members():
                for dx in steps_x:
                    if (dx, dy, dz) not in number:
                        continue
                    if dx == 0 or pair:
                        act((dx, dy, dz))
                    else:
                        pl.when(present((sign * dx, 0, 0)))(lambda: act((dx, dy, dz)))
            if dy == 0 and dz == 0:
                members()
            else:
                pl.when(present((0, sign * dy, sign * dz)))(members)

    cs[0] = jnp.zeros(cs.shape[1:], F32)
    loads = [
        pltpu.make_async_copy(
            ref, cs.at[0, f, pl.ds(DEPTH, bx), pl.ds(2 * ROWS, by)], load_sem.at[f]
        )
        for f, ref in ((0, c_ref), (1, s_ref))
    ]
    for load in loads:
        load.start()
    fresh[...] = jnp.zeros_like(fresh)
    land_cs[...] = jnp.zeros_like(land_cs)
    land_v[...] = jnp.zeros_like(land_v)

    barrier = pltpu.get_barrier_semaphore()
    total = jnp.int32(0)
    for o in number:
        ok = present((0, o[1], o[2]) if pair else o)
        total = total + (1 if ok is None else ok.astype(jnp.int32))
    each(
        flat_groups + deep_groups,
        lambda o: pl.semaphore_signal(
            barrier, inc=1, device_id=device(o), device_id_type=MESH
        ),
    )

    for k in range(nz):
        far = jnp.abs(mz - k) >= 2
        total = total + far.astype(jnp.int32)

        @pl.when(far)
        def _():
            pl.semaphore_signal(
                barrier, inc=1, device_id={"gx": mx, "gy": my, "gz": k}, device_id_type=MESH
            )

    for i in range(nx):
        for j in range(ny):
            far = (jnp.abs(mx - i) >= 2) | (jnp.abs(my - j) >= 2)
            total = total + far.astype(jnp.int32)

            @pl.when(far)
            def _():
                pl.semaphore_signal(
                    barrier, inc=1, device_id={"gx": i, "gy": j, "gz": mz}, device_id_type=MESH
                )

    spread[...] = jnp.zeros_like(spread)
    for ref in (work_a, work_b, cs.at[1, 0]):
        lead = ref.shape[:-2]
        ref[..., 0:ROWS, :] = jnp.zeros(lead + (ROWS, LANES), F32)
        ref[..., ROWS + py:, :] = jnp.zeros(lead + (ROWS, LANES), F32)
    for load in loads:
        load.wait()
    pl.semaphore_wait(barrier, total)

    lane = lax.broadcasted_iota(jnp.int32, (py, LANES), 1)
    lane_by = lax.broadcasted_iota(jnp.int32, (by, LANES), 1)

    def x_ranges(dx, incoming):
        if dx == 0:
            return pl.ds(DEPTH, bx), pl.ds(DEPTH, bx), 1
        if pair:
            up = mx if incoming else 1 - mx
            return (
                pl.ds(DEPTH + (bx - DEPTH) * up, DEPTH),
                pl.ds((DEPTH + bx) * (1 - up), DEPTH), 2 * up,
            )
        if dx > 0:
            return pl.ds(bx, DEPTH), pl.ds(0, DEPTH), 2
        return pl.ds(DEPTH, DEPTH), pl.ds(DEPTH + bx, DEPTH), 0

    ys = {0: pl.ds(ROWS, by), 1: pl.ds(by, ROWS), -1: pl.ds(ROWS, ROWS)}
    yd = {0: pl.ds(ROWS, by), 1: pl.ds(0, ROWS), -1: pl.ds(ROWS + by, ROWS)}
    yp = {0: pl.ds(0, by), 1: pl.ds(by - ROWS, ROWS), -1: pl.ds(0, ROWS)}

    def copy(which, o, main, packed, landed, incoming=False):
        dx, dy, dz = o
        source_x, target_x, slot = x_ranges(dx, incoming)
        if dz == 0:
            base = 0 if which else ROWS
            source = main.at[:, source_x, pl.ds(ys[dy].start + base, ys[dy].size)]
            target = main.at[:, target_x, pl.ds(yd[dy].start + base, yd[dy].size)]
        else:
            side = 0 if dz > 0 else 1
            source = packed.at[side, :, yp[dy]]
            target = landed.at[slot, side, :, yd[dy]]
        return pltpu.make_async_remote_copy(
            src_ref=source, dst_ref=target,
            send_sem=send_sem.at[which, number[o]], recv_sem=recv_sem.at[which, number[o]],
            device_id=device(o), device_id_type=MESH,
        )

    def send_flat(which, main, packed, landed):
        each(flat_groups, lambda o: copy(which, o, main, packed, landed).start())

    def send_deep(which, main, packed, landed):
        for f in range(packed.shape[1]):
            right = jnp.zeros((by, LANES), F32)
            left = jnp.zeros((by, LANES), F32)
            for j in range(bx):
                base = ROWS if which else 2 * ROWS
                v = main[f, DEPTH + j, base:base + by]
                here = lane_by // ROWS == j
                right = jnp.where(here, pltpu.roll(v, (ROWS * j + ROWS) % LANES, 1), right)
                left = jnp.where(here, pltpu.roll(v, (ROWS * j) % LANES, 1), left)
            packed[0, f] = right
            packed[1, f] = left
        each(deep_groups, lambda o: copy(which, o, main, packed, landed).start())

    def arrive(which, main, packed, landed):
        each(
            flat_groups + deep_groups,
            lambda o: copy(which, o, main, packed, landed, True).wait_recv(), -1,
        )

    def sent(which, main, packed, landed):
        each(
            flat_groups + deep_groups,
            lambda o: copy(which, o, main, packed, landed).wait_send(),
        )

    def rim_of(landed, f, x):
        if x < DEPTH:
            slot, j = 2, bx - DEPTH + x
        elif x < DEPTH + bx:
            slot, j = 1, x - DEPTH
        else:
            slot, j = 0, x - DEPTH - bx
        before = pltpu.roll(landed[slot, 0, f], (LANES - ROWS - ROWS * j) % LANES, 1)
        after = pltpu.roll(landed[slot, 1, f], (LANES - ROWS * j) % LANES, 1)
        return jnp.where(
            lane < ROWS, after, jnp.where(lane >= LANES - ROWS, before, 0.0)
        )

    flat_me = mx * ny + my

    def others(me, size):
        for o in range(1, size):
            p = me + o
            yield jnp.where(p >= size, p - size, p)

    def line_copy(k, p, slot):
        return pltpu.make_async_remote_copy(
            src_ref=line.at[k, slot], dst_ref=line.at[k, slot],
            send_sem=line_send.at[k, p], recv_sem=line_recv.at[k, slot],
            device_id={"gx": mx, "gy": my, "gz": p}, device_id_type=MESH,
        )

    def plane_copy(k, q, slot):
        return pltpu.make_async_remote_copy(
            src_ref=plane.at[k, slot], dst_ref=plane.at[k, slot],
            send_sem=plane_send.at[k, q], recv_sem=plane_recv.at[k, slot],
            device_id={"gx": q // ny, "gy": q % ny, "gz": mz}, device_id_type=MESH,
        )

    def restrict_send(k, sums):
        row = lax.broadcasted_iota(jnp.int32, (ypad, LANES), 0)
        parts = []
        for a in range(cx):
            out = jnp.zeros((ypad, LANES), F32)
            for b in range(cy):
                t = jnp.sum(sums[a][b * COARSE:(b + 1) * COARSE], axis=0, keepdims=True)
                out = jnp.where(row == my * cy + b, t, out)
            parts.append(out)
        tall = jnp.concatenate(parts, axis=0)
        fine = lax.broadcasted_iota(jnp.int32, (bz, LANES), 0)
        cell = lax.broadcasted_iota(jnp.int32, (bz, LANES), 1)
        place = (cell == mz * cz + fine // COARSE).astype(F32)
        tall = jnp.dot(tall, place, preferred_element_type=F32, precision=HIGH)
        line[k, mz] = tall.reshape(cx, ypad, LANES)
        for p in others(mz, nz):
            line_copy(k, p, mz).start()

    def gather_middle(k):
        for p in others(mz, nz):
            line_copy(k, p, p).wait_recv()
        acc = line[k, 0]
        for p in range(1, nz):
            acc = acc + line[k, p]
        plane[k, flat_me] = acc
        for q in others(flat_me, nx * ny):
            plane_copy(k, q, flat_me).start()

    def gather_end(k):
        for q in others(flat_me, nx * ny):
            plane_copy(k, q, q).wait_recv()
        parts = []
        for i in range(nx):
            acc = plane[k, i * ny]
            for j in range(1, ny):
                acc = acc + plane[k, i * ny + j]
            parts.append(acc)
        return jnp.concatenate(parts, axis=0)

    def line_sent(k):
        for p in others(mz, nz):
            line_copy(k, p, mz).wait_send()

    def plane_sent(k):
        for q in others(flat_me, nx * ny):
            plane_copy(k, q, flat_me).wait_send()

    body_rows = pl.ds(ROWS, py)

    def six(ref, x, size):
        planes = [[ref[p, x - 1 + i, body_rows] for i in range(size + 2)] for p in (0, 1)]
        out = []
        for i in range(1, size + 1):
            main, rim = planes[0][i], planes[1][i]
            m_up, m_down = pltpu.roll(main, 1, 1), pltpu.roll(main, LANES - 1, 1)
            r_up, r_down = pltpu.roll(rim, 1, 1), pltpu.roll(rim, LANES - 1, 1)
            first, last = lane == 0, lane == LANES - 1
            ends = (
                (jnp.where(first, r_up, m_up), jnp.where(last, r_down, m_down)),
                (jnp.where(first, m_up, r_up), jnp.where(last, m_down, r_down)),
            )
            for p in (0, 1):
                near = (
                    planes[p][i - 1], planes[p][i + 1],
                    ref[p, x - 1 + i, pl.ds(ROWS - 1, py)],
                    ref[p, x - 1 + i, pl.ds(ROWS + 1, py)],
                ) + ends[p]
                out.append((p, x - 1 + i, planes[p][i], near))
        return out

    def group_of(count):
        return max(g for g in range(1, 7) if count % g == 0)

    def sweep(source, target, margin):
        if margin > 1 and group_of(px - 2 * margin) < 3:
            margin = margin - 1
        count = px - 2 * margin
        size = group_of(count)

        def step(g, carry):
            for part, x, v, near in six(source, margin + g * size, size):
                acc = (1.0 - OMEGA) * v + coef[6, part, x]
                for n in range(6):
                    acc = acc + coef[n, part, x] * near[n]
                target[part, x, body_rows] = acc
            return carry
        lax.fori_loop(0, count // size, step, 0)

    def core(source, x, weight):
        inner = pl.ds(2 * ROWS, by)
        own = pl.ds(ROWS, by)
        mid = source[0, x, inner]
        rim = source[1, x, inner]
        low = jnp.where(lane_by == 0, pltpu.roll(rim, 1, 1), pltpu.roll(mid, 1, 1))
        high = jnp.where(
            lane_by == LANES - 1, pltpu.roll(rim, LANES - 1, 1), pltpu.roll(mid, LANES - 1, 1)
        )
        near = (
            source[0, x - 1, inner], source[0, x + 1, inner],
            source[0, x, pl.ds(2 * ROWS - 1, by)], source[0, x, pl.ds(2 * ROWS + 1, by)],
            low, high,
        )
        acc = weight * mid + coef[6, 0, x, own]
        for n in range(6):
            acc = acc + coef[n, 0, x, own] * near[n]
        return acc

    both = cs.at[0]
    send_flat(0, both, pack_cs, land_cs)
    send_deep(0, both, pack_cs, land_cs)

    sums = []
    for a in range(cx):
        acc = jnp.zeros((by, LANES), F32)
        for t in range(COARSE):
            acc = acc + cs[0, 0, DEPTH + a * COARSE + t, 2 * ROWS:2 * ROWS + by]
        sums.append(acc * (1.0 / (COARSE * COARSE)))
    restrict_send(0, sums)
    gather_middle(0)
    arrive(0, both, pack_cs, land_cs)

    for f in range(2):
        for x in range(px):
            cs[1, f, x, body_rows] = rim_of(land_cs, f, x)

    size = group_of(px - 2)

    def make(g, carry):
        for part, x, c, near in six(cs.at[:, 0], 1 + g * size, size):
            faces = [0.5 * (c + n) for n in near]
            diag = (faces[0] + faces[1]) + (faces[2] + faces[3]) + (faces[4] + faces[5])
            here = c > 0.0
            w = jnp.where(here, OMEGA / jnp.where(here, diag, 1.0), 0.0)
            for n in range(6):
                coef[n, part, x] = w * faces[n]
            first = w * cs[part, 1, x, body_rows]
            coef[6, part, x] = first
            work_a[part, x, body_rows] = first
            if part == 0:
                scale[x] = (1.0 / OMEGA) * diag
        return carry
    lax.fori_loop(0, (px - 2) // size, make, 0)

    for cycle in range(CYCLES):
        if cycle == 0:
            order, first = [(work_a, work_b), (work_b, work_a), (work_a, work_b)], 2
        else:
            order, first = [(work_a, work_b), (work_b, work_a)] * 2, 1
        for i, (source, target) in enumerate(order):
            sweep(source, target, first + i)
        last = order[-1][1]
        which = 1 + 2 * cycle
        slot = which - 1
        main, packed, landed = fresh.at[slot], pack_v.at[slot], land_v.at[slot]
        fresh[slot, 0, DEPTH:DEPTH + bx, ROWS:ROWS + by] = (
            last[0, DEPTH:DEPTH + bx, 2 * ROWS:2 * ROWS + by]
        )

        sums = []
        for a in range(cx):
            acc = jnp.zeros((by, LANES), F32)
            for x in range(DEPTH + a * COARSE, DEPTH + a * COARSE + COARSE):
                acc = acc + core(last, x, -OMEGA) * scale[x, ROWS:ROWS + by]
            sums.append(acc)
        restrict_send(1 + cycle, sums)
        send_flat(which, main, packed, landed)
        send_deep(which, main, packed, landed)
        gather_middle(1 + cycle)

        line_sent(1 + cycle)
        if cycle == 0:
            sent(0, both, pack_cs, land_cs)
            line_sent(0)
            plane_sent(0)
        else:
            plane_sent(cycle)
        sent(which, main, packed, landed)
        arrive(which, main, packed, landed)
        for x in range(px):
            work_a[1, x, body_rows] = rim_of(land_v.at[slot], 0, x)

        if cycle == 0:
            cc = gather_end(0)
            shape = cc.shape
            row = lax.broadcasted_iota(jnp.int32, shape, 1)
            col = lax.broadcasted_iota(jnp.int32, shape, 2)
            blank = jnp.zeros((1,) + shape[1:], F32)

            def shifts(v):
                return (
                    jnp.concatenate([blank, v[:-1]], axis=0),
                    jnp.concatenate([v[1:], blank], axis=0),
                    jnp.where(row == 0, 0.0, pltpu.roll(v, 1, 1)),
                    jnp.where(row == shape[1] - 1, 0.0, pltpu.roll(v, shape[1] - 1, 1)),
                    jnp.where(col == 0, 0.0, pltpu.roll(v, 1, 2)),
                    jnp.where(col == LANES - 1, 0.0, pltpu.roll(v, LANES - 1, 2)),
                )

            faces = [0.5 * (cc + n) for n in shifts(cc)]
            diag = (faces[0] + faces[1]) + (faces[2] + faces[3]) + (faces[4] + faces[5])
            here = cc > 0.0
            w = jnp.where(here, OMEGA / jnp.where(here, diag, 1.0), 0.0)
            for n in range(6):
                coarse[n] = w * faces[n]
            coarse[6] = w

        rhs = gather_end(1 + cycle) * coarse[6]
        corr = rhs
        for _ in range(CSWEEPS - 1):
            acc = (1.0 - OMEGA) * corr + rhs
            for n, v in enumerate(shifts(corr)):
                acc = acc + coarse[n] * v
            corr = acc

        tall = corr.reshape(-1, LANES)
        cell = lax.broadcasted_iota(jnp.int32, (LANES, LANES), 0)
        fine = lax.broadcasted_iota(jnp.int32, (LANES, LANES), 1)
        to_main = (cell == mz * cz + fine // COARSE).astype(F32)
        to_rim = (
            ((fine < ROWS) & (cell == mz * cz + cz))
            | ((fine >= LANES - ROWS) & (cell == mz * cz - 1))
        ).astype(F32)
        for part, matrix in ((0, to_main), (1, to_rim)):
            wide = jnp.dot(tall, matrix, preferred_element_type=F32, precision=HIGH)
            spread[part, 1:1 + shape[0], ROWS:ROWS + shape[1]] = wide.reshape(shape)

        def lifted(part, x):
            a = mx * cx + 1 + (x - DEPTH) // COARSE
            rows = []
            for t in range(py // ROWS):
                one = spread[part, a, pl.ds(ROWS - 1 + my * cy + t, 1)]
                rows.append(jnp.broadcast_to(one, (ROWS, LANES)))
            return jnp.concatenate(rows, axis=0)

        lifts = {}
        for x in range(px):
            key = (x - DEPTH) // COARSE
            if key not in lifts:
                lifts[key] = (lifted(0, x), lifted(1, x))
        for x in range(px):
            key = (x - DEPTH) // COARSE
            work_a[0, x, body_rows] = fresh[slot, 0, x] + lifts[key][0]
            work_a[1, x, body_rows] = work_a[1, x, body_rows] + lifts[key][1]

        sweep(work_a, work_b, 1)
        sweep(work_b, work_a, 2)
        sweep(work_a, work_b, 3)
        if cycle == CYCLES - 1:
            for x in range(DEPTH, DEPTH + bx):
                o_ref[x - DEPTH] = core(work_b, x, 1.0 - OMEGA)
        else:
            which, slot = which + 1, slot + 1
            main, packed, landed = fresh.at[slot], pack_v.at[slot], land_v.at[slot]

            for x in range(DEPTH, DEPTH + bx):
                fresh[slot, 0, x, ROWS:ROWS + by] = core(work_b, x, 1.0 - OMEGA)
            send_flat(which, main, packed, landed)
            send_deep(which, main, packed, landed)
            sent(which, main, packed, landed)
            arrive(which, main, packed, landed)
            for x in range(px):
                work_a[0, x, body_rows] = fresh[slot, 0, x]
                work_a[1, x, body_rows] = rim_of(land_v.at[slot], 0, x)

    plane_sent(CYCLES)


def body(counts, right_side, conductivity):
    nx, ny, nz = counts
    bx, by, bz = block = right_side.shape
    assert bz == LANES and bx * ROWS <= LANES and bx % COARSE == 0 and by % COARSE == 0
    assert nz * bz // COARSE <= LANES
    px, py = bx + 2 * DEPTH, by + 2 * ROWS
    cx = bx // COARSE
    ypad = -(-(ny * by // COARSE) // ROWS) * ROWS
    moves = 2 * CYCLES - 1
    vmem = pltpu.VMEM
    dma = pltpu.SemaphoreType.DMA
    return pl.pallas_call(
        functools.partial(kernel, counts, block),
        out_shape=jax.ShapeDtypeStruct(block, F32),
        in_specs=[pl.BlockSpec(memory_space=pltpu.HBM)] * 2,
        out_specs=pl.BlockSpec(memory_space=vmem),
        scratch_shapes=[
            vmem((2, 2, px, py + 2 * ROWS, LANES), F32),
            vmem((moves, 1, px, py, LANES), F32),
            vmem((2, px, py + 2 * ROWS, LANES), F32),
            vmem((2, px, py + 2 * ROWS, LANES), F32),
            vmem((7, 2, px, py, LANES), F32),
            vmem((px, py, LANES), F32),
            vmem((2, 2, by, LANES), F32),
            vmem((3, 2, 2, py, LANES), F32),
            vmem((moves, 2, 1, by, LANES), F32),
            vmem((moves, 3, 2, 1, py, LANES), F32),
            vmem((CYCLES + 1, nz, cx, ypad, LANES), F32),
            vmem((CYCLES + 1, nx * ny, cx, ypad, LANES), F32),
            vmem((7, nx * cx, ypad, LANES), F32),
            vmem((2, nx * cx + 2, ypad + 2 * ROWS, LANES), F32),
            dma((2,)),
            dma((moves + 1, 26)),
            dma((moves + 1, 26)),
            dma((CYCLES + 1, nz)),
            dma((CYCLES + 1, nz)),
            dma((CYCLES + 1, nx * ny)),
            dma((CYCLES + 1, nx * ny)),
        ],
        compiler_params=pltpu.CompilerParams(
            collective_id=0, has_side_effects=True, vmem_limit_bytes=60 * 1024 * 1024
        ),
    )(right_side, conductivity)


def solution(mesh):
    counts = tuple(mesh.shape[name] for name in ("gx", "gy", "gz"))
    return jax.shard_map(
        functools.partial(body, counts),
        mesh=mesh,
        in_specs=(P("gx", "gy", "gz"), P("gx", "gy", "gz")),
        out_specs=P("gx", "gy", "gz"),
        check_vma=False,
    )
```
